128 devices in a mesh: ctx: 16 (over z_lo, y, core), resp: 8 (over x, z_hi).
Axes of the slice: x: 4, y: 4, z: 4 (z_hi: 2, z_lo: 2; z = z_hi * 2 + z_lo), core: 2. Of those that a mesh axis runs over, the one named last changes fastest.
Arguments:
- queries: bfloat16 [8, 512, 36864], P('resp', None, 'ctx'), may hold values from -6 to 6
- attn_cot: bfloat16 [8, 512, 32768], P('resp', None, 'ctx'), may hold values from -24 to 24
- prompt_latent: bfloat16 [1024, 576], P('ctx'), may hold values from -6 to 6
- response_latent: bfloat16 [8, 512, 576], P('resp'), may hold values from -6 to 6
- log_ratio: float32 [8, 512], P('resp'), may hold values from -0.6 to 0.6
- lengths: int32 [8, 2], P('resp'), may hold values from 64 to 256, as said below
- chosen: int32 [8], P('resp'), may hold values from 0 to 1
- moe_cot: bfloat16 [8, 512, 7168], P('resp', 'ctx'), may hold values from -24 to 24
- expert_ids: int32 [8, 512, 8], P('resp', 'ctx'), may hold values from 0 to 255, all different within a row; in each aligned block of 32 rows (0 to 31, 32 to 63, ..., all dimensions but the last counted through in order) at most 2 rows name the same one
- router_logits: float32 [8, 512, 8], P('resp', 'ctx'), may hold values from -6 to 6
- expert_outputs: bfloat16 [128, 256, 2, 7168], P(None, ('ctx', 'resp')), may hold values from -0.1796875 to 0.1796875
Outputs:
- grad_query: bfloat16 [8, 512, 36864], P('resp', None, 'ctx')
- grad_prompt: float32 [1024, 576], P(('ctx', 'resp'))
- grad_response: float32 [8, 512, 576], P('resp', 'ctx')
- expert_row_grads: bfloat16 [128, 256, 2, 7168], P(None, ('ctx', 'resp'))
- grad_router: float32 [8, 512, 8], P('resp', 'ctx')
The draws below stay inside these ranges and needn't reach their ends.
Inputs may be any that keep to these rules, and one draw needn't show every extreme that they name: `lengths`: every draw has a response of length 256 and one of length 64. `expert_ids`: each row names 8 different experts; among the rows of one device no expert is named more than 2 times, and in every draw some device's rows name some expert exactly 2 times.
All inputs are finite; a program needn't handle non-finite values.
Results may differ from the reference program's by a relative error of at most 0.012.
The reference program's roundings to bfloat16 on the way count: a program that leaves them out, or rounds other values in their place, can miss the bound.
Values may be sent and summed in bfloat16 or wider, within the bound.
No kernel may reach another device: no remote copies, remote signals or barrier semaphores. Data moves between devices by JAX's collectives and lax.ppermute only.
A program may use at most 192 MiB of HBM per device.

```python
import math
import jax
import jax.numpy as jnp
import numpy as np
from jax import lax

D = 7168
H = 64
KV_RANK = 512
LAT = 576
EXPERTS = 256
TOP = 8
CAP = 2
R_LEN = 256
PAIRS = 8
PROMPT = 1024
M_DEV = 32
N_CTX = 16
N_RESP = 8


def draw_queries(key, part):
    key = jax.random.fold_in(key, 1)
    layout = (PAIRS, 2 * R_LEN, H, LAT)
    values = jnp.clip(jax.random.normal(key, layout, jnp.float32), -6.0, 6.0)
    return values.reshape(PAIRS, 2 * R_LEN, H * LAT).astype(jnp.bfloat16)


def draw_prompt_latent(key, part):
    key = jax.random.fold_in(key, 2)
    layout = (PROMPT, LAT)
    values = jnp.clip(jax.random.normal(key, layout, jnp.float32), -6.0, 6.0)
    return values.astype(jnp.bfloat16)


def draw_lengths(key, part):
    key = jax.random.fold_in(key, 3)
    subkeys = jax.random.split(key, 3)
    entries = 2 * PAIRS
    values = jax.random.randint(subkeys[0], (entries,), R_LEN // 4, R_LEN + 1)
    longest = jax.random.randint(subkeys[1], (), 0, entries)
    shortest = (longest + 1 + jax.random.randint(subkeys[2], (), 0, entries - 1)) % entries
    positions = jnp.arange(entries)
    values = jnp.where(positions == longest, R_LEN, values)
    values = jnp.where(positions == shortest, R_LEN // 4, values)
    return values.reshape(PAIRS, 2).astype(jnp.int32)


def touch_ends(values, stream_key, smallest, high):
    longest = values.shape.index(max(values.shape))
    spots = []
    for shift in (0, 1):
        where = [jax.random.randint(jax.random.fold_in(stream_key, axis), (), 0, length) for axis, length in enumerate(values.shape)]
        where[longest] = (where[longest] + shift) % values.shape[longest]
        spots.append(tuple(where))
    return values.at[spots[0]].set(smallest).at[spots[1]].set(high)


def steps_of(key, shape, cuts, smallest, largest):
    factor_of = 1.0
    for dim, blocks in cuts:
        draws = jax.random.uniform(jax.random.fold_in(jax.random.fold_in(key, 6), dim), (blocks,), jnp.float32, smallest / len(cuts), largest / len(cuts))
        factor_of = factor_of * jnp.repeat(jnp.exp(draws), shape[dim] // blocks).reshape((-1,) + (1,) * (len(shape) - 1 - dim))
    return factor_of


def routed_block(rng, own, number, rows, count, top, bound, slope):
    ranking = jax.random.permutation(rng, count)
    crowded, usual = portions_of(count, rows * top, bound, slope, True), portions_of(count, rows * top, bound, slope, False)
    places = jnp.arange(count)

    def named(sizes, rotation):
        used = int((sizes > 0).sum())
        fixed = max(1, used // 4)
        moved = fixed + (places - fixed + rotation * (used - fixed)) % max(1, count - fixed)
        return jnp.zeros((count,), jnp.int32).at[ranking[jnp.where(places < fixed, places, moved)]].set(jnp.asarray(sizes, jnp.int32))

    sizes = jnp.where(number % 4 == 0, named(crowded, number // 4), named(usual, number - number // 4 - 1))
    mixed = jax.random.permutation(jax.random.fold_in(own, 3), count)
    giver, taker = mixed[0:count // 2 * 2:2], mixed[1:count // 2 * 2:2]
    slack = jnp.minimum(sizes[giver] - 1, bound - sizes[taker]) // 2
    slack = jnp.where((giver == ranking[0]) | (taker == ranking[0]) | (sizes[taker] == 0), 0, jnp.maximum(slack, 0))
    moved = jax.random.randint(jax.random.fold_in(own, 4), (count // 2,), 0, 1 << 20) % (slack + 1)
    sizes = sizes.at[giver].add(-moved).at[taker].add(moved)
    members = jnp.searchsorted(jnp.cumsum(sizes), jnp.arange(rows * top), side="right").astype(jnp.int32)
    listing = members.reshape(top, rows).T
    listing = listing[jax.random.permutation(jax.random.fold_in(own, 1), rows)]
    rotation = jax.random.randint(jax.random.fold_in(own, 2), (rows, 1), 0, top)
    return jnp.take_along_axis(listing, (jnp.arange(top)[None, :] + rotation) % top, axis=1)


def portions_of(number_of, total, bound, lean, full):
    loads = [(1 << 20) // math.isqrt(rank ** lean) + 1 for rank in range(1, number_of + 1)]
    largest = bound if full else min(bound, max(-(-total // number_of), total * loads[0] // sum(loads)))
    least = 1 if total - largest >= number_of - 1 else 0
    holding, rest = [largest] + [least] * (number_of - 1), total - largest - least * (number_of - 1)
    while rest > 0:
        free = [i for i in range(1, number_of) if holding[i] < largest] or [i for i in range(1, number_of) if holding[i] < bound]
        pool, left = sum([loads[i] for i in free]), rest
        for i in free:
            more = min(bound - holding[i], max(1, left * loads[i] // pool), rest)
            holding[i] = holding[i] + more
            rest = rest - more
    return np.array(holding)


def gaussian(own_key, dims, spread, most, shards=(), kind=jnp.bfloat16):
    values = spread * jax.random.normal(own_key, dims, jnp.float32)
    if shards:
        values = values * steps_of(own_key, dims, shards, -0.22, 0.18)
    return jnp.clip(values, -most, most).astype(kind)


def setup_inputs(seed: int = 0) -> dict:
    keys = jax.random.split(jax.random.key(seed), 12)
    queries = draw_queries(jax.random.fold_in(keys[11], 71), 0)
    attn_cot = gaussian(keys[1], (PAIRS, 2 * R_LEN, H * KV_RANK), 4.0, 24.0, ((0, 8), (2, 16)))
    prompt_latent = draw_prompt_latent(jax.random.fold_in(keys[11], 71), 0)
    response_latent = gaussian(keys[3], (PAIRS, 2 * R_LEN, LAT), 1.0, 6.0, ((0, 8),))
    log_ratio = gaussian(keys[4], (PAIRS, 2 * R_LEN), 0.1, 0.6, ((0, 8),), jnp.float32)
    lengths = draw_lengths(jax.random.fold_in(keys[11], 71), 0)
    chosen = touch_ends(jax.random.randint(keys[6], (PAIRS,), 0, 2), jax.random.fold_in(keys[6], 1), 0, 1).astype(jnp.int32)
    moe_cot = gaussian(keys[7], (PAIRS, 2 * R_LEN, D), 4.0, 24.0, ((0, 8), (1, 16)))
    expert_ids_keys = jax.random.split(jax.random.fold_in(keys[8], 1), PAIRS * (2 * R_LEN) // M_DEV)
    expert_ids_turns = jax.random.permutation(jax.random.fold_in(keys[8], 3), PAIRS * (2 * R_LEN) // M_DEV)
    expert_ids = jax.vmap(lambda own, number: routed_block(jax.random.fold_in(keys[8], 2), own, number, M_DEV, EXPERTS, TOP, CAP, 2))(expert_ids_keys, expert_ids_turns).reshape((PAIRS, 2 * R_LEN, TOP))
    router_logits = gaussian(keys[9], (PAIRS, 2 * R_LEN, TOP), 1.5, 6.0, ((0, 8), (1, 16)), jnp.float32)
    expert_outputs = gaussian(keys[10], (N_CTX * N_RESP, EXPERTS, CAP, D), 0.03, 0.1796875, ((1, 128),))
    return {"queries": queries, "attn_cot": attn_cot, "prompt_latent": prompt_latent, "response_latent": response_latent, "log_ratio": log_ratio, "lengths": lengths, "chosen": chosen, "moe_cot": moe_cot, "expert_ids": expert_ids, "router_logits": router_logits, "expert_outputs": expert_outputs}


score_scale = 192.0 ** -0.5
preference_beta = 0.5
route_scale = 2.5


def pair_coefficients(log_ratio, lengths, chosen):
    pair_count = log_ratio.shape[0]
    half_rows = log_ratio.shape[1] // 2
    position = jnp.arange(half_rows, dtype=jnp.int32)
    live_mask = position[None, None, :] < lengths[:, :, None]
    ratios = log_ratio.reshape(pair_count, 2, half_rows)
    totals = jnp.sum(jnp.where(live_mask, ratios, jnp.zeros_like(ratios)), axis=2)
    margin = jnp.where(chosen == 0, totals[:, 0] - totals[:, 1], totals[:, 1] - totals[:, 0])
    weight = preference_beta * jax.nn.sigmoid(-preference_beta * margin)
    member = jnp.arange(2, dtype=jnp.int32)
    signed = jnp.where(member[None, :] == chosen[:, None], -weight[:, None], weight[:, None])
    return (signed[:, :, None] * live_mask.astype(signed.dtype)).reshape(pair_count, 2 * half_rows)


def allowed_keys(row_count, prompt_count):
    half_rows = row_count // 2
    query_index = jnp.arange(row_count, dtype=jnp.int32)[:, None]
    column_index = jnp.arange(prompt_count + row_count, dtype=jnp.int32)[None, :] - prompt_count
    same_answer = (column_index >= 0) & (column_index // half_rows == query_index // half_rows) & (column_index <= query_index)
    return (column_index < 0) | same_answer


def head_grads(query, cot_head, key_rows, row_coef, allowed):
    rank = cot_head.shape[1]
    scores = jnp.dot(query, key_rows.T, preferred_element_type=jnp.float32) * score_scale
    scores = jnp.where(allowed, scores, -jnp.inf)
    row_top = jnp.max(scores, axis=1, keepdims=True)
    exponent = jnp.exp(scores - row_top)
    soft_weights = exponent / jnp.sum(exponent, axis=1, keepdims=True)
    soft_rounded = soft_weights.astype(jnp.bfloat16)
    values = key_rows[:, :rank]
    grad_out = (row_coef[:, None] * cot_head.astype(jnp.float32)).astype(jnp.bfloat16)
    attn_out = jnp.dot(soft_rounded, values, preferred_element_type=jnp.float32)
    row_delta = jnp.sum(grad_out.astype(jnp.float32) * attn_out, axis=1, keepdims=True)
    prob_grad = jnp.dot(grad_out, values.T, preferred_element_type=jnp.float32)
    score_grad = (soft_weights * (prob_grad - row_delta)).astype(jnp.bfloat16)
    grad_query = (score_scale * jnp.dot(score_grad, key_rows, preferred_element_type=jnp.float32)).astype(jnp.bfloat16)
    key_grad = score_scale * jnp.dot(score_grad.T, query, preferred_element_type=jnp.float32)
    value_grad = jnp.dot(soft_rounded.T, grad_out, preferred_element_type=jnp.float32)
    key_grad = key_grad + jnp.pad(value_grad, ((0, 0), (0, key_rows.shape[1] - rank)))
    return grad_query, key_grad


def source_block(inputs):
    cot_rows, id_rows, logit_rows, coef_rows, saved_rows = inputs
    grad_rows = (coef_rows[:, None] * cot_rows.astype(jnp.float32)).astype(jnp.bfloat16)
    affinity = jax.nn.sigmoid(logit_rows)
    total = jnp.sum(affinity, axis=1, keepdims=True)
    gate = route_scale * affinity / total
    gate_low = gate.astype(jnp.bfloat16)
    flat_ids = id_rows.reshape(-1)
    entries = flat_ids.shape[0]
    order = jnp.arange(entries, dtype=jnp.int32)
    earlier = (flat_ids[None, :] == flat_ids[:, None]) & (order[None, :] < order[:, None])
    slot_index = jnp.sum(earlier.astype(jnp.int32), axis=1)
    placing = flat_ids * CAP + slot_index
    owner_row = order // TOP
    picked = jnp.take(grad_rows, owner_row, axis=0)
    scaled = (gate_low.reshape(-1)[:, None].astype(jnp.float32) * picked.astype(jnp.float32)).astype(jnp.bfloat16)
    block = jnp.zeros((EXPERTS * CAP, D), jnp.bfloat16).at[placing].set(scaled).reshape(EXPERTS, CAP, D)
    stored = jnp.take(saved_rows.reshape(EXPERTS * CAP, D), placing, axis=0)
    gate_grad = jnp.sum(picked.astype(jnp.float32) * stored.astype(jnp.float32), axis=1).reshape(id_rows.shape)
    mixed = jnp.sum(gate_grad * affinity, axis=1, keepdims=True) / total
    router_grad = route_scale / total * (gate_grad - mixed) * affinity * (1.0 - affinity)
    return block, router_grad


def reference(queries, attn_cot, prompt_latent, response_latent, log_ratio, lengths, chosen, moe_cot, expert_ids, router_logits, expert_outputs):
    coefficient = pair_coefficients(log_ratio, lengths, chosen)
    row_count = 2 * R_LEN
    allowed = allowed_keys(row_count, PROMPT)

    def pair_step(prompt_sum, inputs):
        query_rows, cot_rows, answer_rows, row_coef = inputs
        key_rows = jnp.concatenate([prompt_latent, answer_rows], axis=0)
        head_queries = query_rows.reshape(row_count, H, LAT).transpose(1, 0, 2)
        head_cots = cot_rows.reshape(row_count, H, KV_RANK).transpose(1, 0, 2)

        def head_step(key_sum, head_inputs):
            grad_head, key_grad = head_grads(head_inputs[0], head_inputs[1], key_rows, row_coef, allowed)
            return key_sum + key_grad, grad_head

        start_sum = jnp.zeros((PROMPT + row_count, LAT), jnp.float32)
        key_sum, head_query_grads = lax.scan(head_step, start_sum, (head_queries, head_cots))
        grad_rows = head_query_grads.transpose(1, 0, 2).reshape(row_count, H * LAT)
        return prompt_sum + key_sum[:PROMPT], (grad_rows, key_sum[PROMPT:])

    grad_prompt, (grad_query, grad_response) = lax.scan(
        pair_step, jnp.zeros((PROMPT, LAT), jnp.float32), (queries, attn_cot, response_latent, coefficient))

    sources = N_CTX * N_RESP

    def to_sources(array):
        trailing = array.shape[2:]
        moved = array.reshape((PAIRS, N_CTX, M_DEV) + trailing)
        moved = moved.transpose((1, 0, 2) + tuple(range(3, 3 + len(trailing))))
        return moved.reshape((sources, M_DEV) + trailing)

    blocks, router_blocks = lax.map(source_block, (to_sources(moe_cot), to_sources(expert_ids), to_sources(router_logits), to_sources(coefficient), expert_outputs))
    grad_router = router_blocks.reshape(N_CTX, PAIRS, M_DEV, TOP).transpose(1, 0, 2, 3).reshape(PAIRS, 2 * R_LEN, TOP)
    return grad_query, grad_prompt, grad_response, blocks, grad_router
```

```python
import jax
import jax.numpy as jnp
from jax import lax
from jax.experimental import pallas as pl
from jax.experimental.pallas import tpu as pltpu
from jax.sharding import PartitionSpec as P

EXPERTS = 256
CAP = 2
LANES = 128

score_scale = 192.0 ** (-0.5)
preference_beta = 0.5
route_scale = 2.5
log2_e = 1.4426950408889634

f32 = jnp.float32
bf16 = jnp.bfloat16


def coefficient_row(ratio_ref, lengths_ref, chosen_ref):
    rows = ratio_ref.shape[1]
    half = rows // 2
    lane = lax.broadcasted_iota(jnp.int32, (1, rows), 1)
    second = lane >= half
    position = jnp.where(second, lane - half, lane)
    length = jnp.where(second, lengths_ref[0, 1], lengths_ref[0, 0])
    live = position < length
    ratios = jnp.where(live, ratio_ref[...], 0.0)
    first_total = jnp.sum(jnp.where(second, 0.0, ratios), axis=1, keepdims=True)
    second_total = jnp.sum(jnp.where(second, ratios, 0.0), axis=1, keepdims=True)
    chosen = chosen_ref[0]
    margin = first_total - second_total
    margin = jnp.where(chosen == 0, margin, -margin)
    weight = preference_beta * jax.nn.sigmoid(-preference_beta * margin)
    signed = jnp.where(second == (chosen == 1), -weight, weight)
    return jnp.where(live, signed, 0.0)


def column_of(row):
    n = row.shape[1]
    return jnp.transpose(jnp.broadcast_to(row, (8, n)))[:, :1]


def router_gates(logits):
    affinity = jax.nn.sigmoid(logits)
    total = jnp.sum(affinity, axis=0, keepdims=True)
    return affinity, total, route_scale * affinity / total


def send_kernel(
    lengths_ref, chosen_ref, start_ref, ratio_ref, ids_ref, logits_ref, cot_ref,
    send_ref, slot_ref, rows_ref, pair_ref, table_ref, gates_ref, table_smem, gates_smem, sems,
):
    tokens, model = cot_ref.shape
    top = ids_ref.shape[0]
    tiles = model // LANES
    per_step = EXPERTS // pl.num_programs(0)

    @pl.when(pl.program_id(0) == 0)
    def _():
        _, _, gate = router_gates(logits_ref[...])
        gate = gate.astype(bf16).astype(f32)
        ids = jnp.transpose(ids_ref[...])
        gates = jnp.transpose(gate)
        expert = lax.broadcasted_iota(jnp.int32, (tokens, EXPERTS), 1)
        named = jnp.zeros((tokens, EXPERTS), f32)
        weight = jnp.zeros((tokens, EXPERTS), f32)
        for n in range(top):
            hit = ids[:, n : n + 1] == expert
            named = jnp.where(hit, 1.0, named)
            weight = jnp.where(hit, gates[:, n : n + 1], weight)
        row_i = lax.broadcasted_iota(jnp.int32, (tokens, tokens), 0)
        col_i = lax.broadcasted_iota(jnp.int32, (tokens, tokens), 1)
        before = jnp.dot(
            (col_i < row_i).astype(bf16), named.astype(bf16), preferred_element_type=f32
        )
        token = lax.broadcasted_iota(jnp.int32, (tokens, EXPERTS), 0).astype(f32)
        for s in range(CAP):
            here = jnp.where((before == float(s)) & (named > 0.0), 1.0, 0.0)
            table_ref[s : s + 1, :] = jnp.sum(here * token, axis=0, keepdims=True).astype(jnp.int32)
            gates_ref[s : s + 1, :] = jnp.sum(here * weight, axis=0, keepdims=True)
        table_copy = pltpu.make_async_copy(table_ref, table_smem, sems.at[0])
        gates_copy = pltpu.make_async_copy(gates_ref, gates_smem, sems.at[1])
        table_copy.start()
        gates_copy.start()
        slots = []
        for n in range(top):
            hit = ids[:, n : n + 1] == expert
            slots.append(jnp.sum(jnp.where(hit, before, 0.0), axis=1, keepdims=True))
        slot_ref[...] = jnp.transpose(jnp.concatenate(slots, axis=1)).astype(jnp.int32)
        coefficient = coefficient_row(ratio_ref, lengths_ref, chosen_ref)
        lane = lax.broadcasted_iota(jnp.int32, (tokens, coefficient.shape[1]), 1)
        row = lax.broadcasted_iota(jnp.int32, (tokens, coefficient.shape[1]), 0)
        own = jnp.sum(
            jnp.where(lane == row + start_ref[0], coefficient, 0.0), axis=1, keepdims=True
        )
        for tile in range(tiles):
            cot = cot_ref[:, tile * LANES : (tile + 1) * LANES].astype(f32)
            rows_ref[pl.ds(tile, tokens, stride=tiles), :] = (own * cot).astype(bf16).astype(f32)
        table_copy.wait()
        gates_copy.wait()

    first = pl.program_id(0) * per_step

    def place(e, carry):
        for s in range(CAP):
            token = table_smem[s, first + e]
            block = rows_ref[pl.ds(pl.multiple_of(token * tiles, 8), tiles), :]
            pair_ref[pl.ds(s, tiles, stride=CAP), :] = block * gates_smem[s, first + e]
        at = pl.multiple_of(e * (tiles * CAP), 16)
        send_ref[pl.ds(at, tiles * CAP), :] = pair_ref[...].astype(bf16)
        return carry

    lax.fori_loop(0, per_step, place, 0, unroll=4)


def build_send(lengths, chosen, start, ratio, ids, logits, cot):
    tokens, model = cot.shape
    tiles = model // LANES
    rows = EXPERTS * CAP * tiles
    steps = 8
    whole = lambda shape: pl.BlockSpec(shape, lambda i: (0, 0))
    smem = pl.BlockSpec(memory_space=pltpu.SMEM)
    return pl.pallas_call(
        send_kernel,
        grid=(steps,),
        in_specs=[
            smem, smem, smem,
            whole(ratio.shape), whole(ids.shape), whole(logits.shape), whole(cot.shape),
        ],
        out_specs=[
            pl.BlockSpec((rows // steps, LANES), lambda i: (i, 0)),
            whole(ids.shape),
        ],
        out_shape=[
            jax.ShapeDtypeStruct((rows, LANES), bf16),
            jax.ShapeDtypeStruct(ids.shape, jnp.int32),
        ],
        scratch_shapes=[
            pltpu.VMEM((tokens * tiles, LANES), f32),
            pltpu.VMEM((tiles * CAP, LANES), f32),
            pltpu.VMEM((8, EXPERTS), jnp.int32),
            pltpu.VMEM((8, EXPERTS), f32),
            pltpu.SMEM((8, EXPERTS), jnp.int32),
            pltpu.SMEM((8, EXPERTS), f32),
            pltpu.SemaphoreType.DMA((2,)),
        ],
        compiler_params=pltpu.CompilerParams(vmem_limit_bytes=32 << 20),
        cost_estimate=pl.CostEstimate(flops=0, bytes_accessed=8_000_000, transcendentals=0),
        name="build_send",
    )(lengths, chosen, start, ratio, ids, logits, cot)


def dot_kernel(got_ref, saved_ref, out_ref):
    rows = got_ref.shape[0]
    pairs = out_ref.shape[0]
    tall = rows // pairs
    product = got_ref[...].astype(f32) * saved_ref[...].astype(f32)
    product = jnp.sum(product.reshape(pairs, tall // 8, 8, LANES), axis=1)
    out_ref[...] = jnp.sum(product, axis=2)


def slot_dots(got, saved, tiles):
    pairs = got.shape[0] // (tiles * CAP)
    steps = 8
    spec = pl.BlockSpec((got.shape[0] // steps, LANES), lambda i: (i, 0))
    return pl.pallas_call(
        dot_kernel,
        grid=(steps,),
        in_specs=[spec, spec],
        out_specs=pl.BlockSpec((pairs // steps, 8), lambda i: (i, 0)),
        out_shape=jax.ShapeDtypeStruct((pairs, 8), f32),
        compiler_params=pltpu.CompilerParams(vmem_limit_bytes=32 << 20),
        cost_estimate=pl.CostEstimate(flops=8_000_000, bytes_accessed=15_000_000, transcendentals=0),
        name="slot_dots",
    )(got, saved)


NT = (((1,), (1,)), ((), ()))


def attention_kernel(
    lengths_ref, chosen_ref, ratio_ref, q_ref, cot_ref, prompt_ref, answer_ref,
    gq_ref, send_ref, keys_ref, keys_t_ref, acc_ref, value_ref,
):
    prompt_count, width = prompt_ref.shape
    row_count = answer_ref.shape[1]
    half = row_count // 2
    wide = keys_ref.shape[2]
    rank = value_ref.shape[1]
    pad = wide - width
    step = pl.program_id(0)

    @pl.when(step == 0)
    def _():
        answer_t = answer_ref[...]
        keys_t_ref[:, :prompt_count] = jnp.transpose(prompt_ref[...])
        keys_t_ref[:, prompt_count:] = answer_t
        latent = jnp.concatenate([prompt_ref[...], jnp.transpose(answer_t)], axis=0)
        zeros = jnp.zeros((latent.shape[0], pad), bf16)
        keys_ref[0] = jnp.concatenate([latent, zeros], axis=1)
        keys_ref[1] = jnp.concatenate([zeros, latent], axis=1)
        acc_ref[...] = jnp.zeros_like(acc_ref)
        value_ref[...] = jnp.zeros_like(value_ref)

    coefficient = column_of(coefficient_row(ratio_ref, lengths_ref, chosen_ref))
    key_i = lax.broadcasted_iota(jnp.int32, (half, half), 0)
    row_i = lax.broadcasted_iota(jnp.int32, (half, half), 1)
    causal = key_i <= row_i
    for k in range(2):
        rows = slice(k * half, (k + 1) * half)
        answer = slice(prompt_count + k * half, prompt_count + (k + 1) * half)
        grads = []
        for h in range(2):
            query = q_ref[rows, h * rank : h * rank + wide]
            grad_out = (
                coefficient[rows] * cot_ref[rows, h * rank : (h + 1) * rank].astype(f32)
            ).astype(bf16)
            s_prompt = lax.dot_general(
                keys_ref[h, :prompt_count], query, NT, preferred_element_type=f32
            )
            s_answer = lax.dot_general(keys_ref[h, answer], query, NT, preferred_element_type=f32)
            s_answer = jnp.where(causal, s_answer, -1e30)
            top = jnp.maximum(
                jnp.max(s_prompt, axis=0, keepdims=True), jnp.max(s_answer, axis=0, keepdims=True)
            )
            e_prompt = jnp.exp2((s_prompt - top) * (score_scale * log2_e))
            e_answer = jnp.exp2((s_answer - top) * (score_scale * log2_e))
            total = jnp.sum(e_prompt, axis=0, keepdims=True) + jnp.sum(
                e_answer, axis=0, keepdims=True
            )
            inverse = 1.0 / total
            p_prompt = e_prompt * inverse
            p_answer = e_answer * inverse
            b_prompt = p_prompt.astype(bf16)
            b_answer = p_answer.astype(bf16)
            d_prompt = lax.dot_general(
                keys_ref[0, :prompt_count, :rank], grad_out, NT, preferred_element_type=f32
            )
            d_answer = lax.dot_general(
                keys_ref[0, answer, :rank], grad_out, NT, preferred_element_type=f32
            )
            delta = jnp.sum(b_prompt.astype(f32) * d_prompt, axis=0, keepdims=True) + jnp.sum(
                b_answer.astype(f32) * d_answer, axis=0, keepdims=True
            )
            g_prompt = (p_prompt * (d_prompt - delta)).astype(bf16)
            g_answer = (p_answer * (d_answer - delta)).astype(bf16)
            grads.append(
                jnp.dot(keys_t_ref[:, :prompt_count], g_prompt, preferred_element_type=f32)
                + jnp.dot(keys_t_ref[:, answer], g_answer, preferred_element_type=f32)
            )
            acc_ref[h, :prompt_count] += jnp.dot(g_prompt, query, preferred_element_type=f32)
            acc_ref[h, answer] += jnp.dot(g_answer, query, preferred_element_type=f32)
            value_ref[:prompt_count] += jnp.dot(b_prompt, grad_out, preferred_element_type=f32)
            value_ref[answer] += jnp.dot(b_answer, grad_out, preferred_element_type=f32)
        both = (score_scale * jnp.concatenate(grads, axis=0)).astype(bf16)
        gq_ref[rows, :] = jnp.transpose(both)

    @pl.when(step == pl.num_programs(0) - 1)
    def _():
        chunks, _, _ = send_ref.shape
        prompt_rows = prompt_count // chunks
        answer_rows = row_count // chunks

        def combined(start, size):
            at = pl.ds(start, size)
            key = acc_ref[0, at, :width] + pltpu.roll(acc_ref[1, at, :], wide - pad, 1)[:, :width]
            value = jnp.concatenate([value_ref[at, :], jnp.zeros((size, width - rank), f32)], axis=1)
            return (score_scale * key + value).astype(bf16)

        for c in range(chunks):
            send_ref[c, :prompt_rows] = combined(c * prompt_rows, prompt_rows)
            send_ref[c, prompt_rows:] = combined(prompt_count + c * answer_rows, answer_rows)


def attention(lengths, chosen, ratio, queries, cot, prompt, answer_t, chunks):
    rows, q_width = queries.shape
    prompt_count, width = prompt.shape
    heads = q_width // width
    rank = cot.shape[1] // heads
    wide = width + width - rank
    steps = heads // 2
    keys = prompt_count + rows
    whole = lambda shape: pl.BlockSpec(shape, lambda i: (0,) * len(shape))
    smem = pl.BlockSpec(memory_space=pltpu.SMEM)
    return pl.pallas_call(
        attention_kernel,
        grid=(steps,),
        in_specs=[
            smem, smem, whole(ratio.shape),
            pl.BlockSpec((rows, 2 * width), lambda i: (0, i)),
            pl.BlockSpec((rows, 2 * rank), lambda i: (0, i)),
            whole(prompt.shape), whole(answer_t.shape),
        ],
        out_specs=[
            pl.BlockSpec((rows, 2 * width), lambda i: (0, i)),
            whole((chunks, keys // chunks, width)),
        ],
        out_shape=[
            jax.ShapeDtypeStruct(queries.shape, bf16),
            jax.ShapeDtypeStruct((chunks, keys // chunks, width), bf16),
        ],
        scratch_shapes=[
            pltpu.VMEM((2, keys, wide), bf16),
            pltpu.VMEM((width, keys), bf16),
            pltpu.VMEM((2, keys, wide), f32),
            pltpu.VMEM((keys, rank), f32),
        ],
        compiler_params=pltpu.CompilerParams(vmem_limit_bytes=50 << 20),
        cost_estimate=pl.CostEstimate(
            flops=17_000_000_000, bytes_accessed=9_000_000, transcendentals=2_600_000
        ),
        name="attention",
    )(lengths, chosen, ratio, queries, cot, prompt, answer_t)


def flat(x):
    n, e, s, d = x.shape
    t = d // LANES
    return x.reshape(n, e, s, t, LANES).transpose(0, 1, 3, 2, 4).reshape(n * e * t * s, LANES)


def unflat(x, n, e, s, d):
    t = d // LANES
    return x.reshape(n, e, t, s, LANES).transpose(0, 1, 3, 2, 4).reshape(n, e, s, d)


def on_device(
    queries,
    attn_cot,
    prompt_latent,
    response_latent,
    log_ratio,
    lengths,
    chosen,
    moe_cot,
    expert_ids,
    router_logits,
    expert_outputs,
):
    ctx_count = lax.axis_size("ctx")
    resp_count = lax.axis_size("resp")
    devices = ctx_count * resp_count
    width = prompt_latent.shape[1]
    tokens, model = moe_cot.shape[1:]
    per_owner = EXPERTS // devices
    start = (lax.axis_index("ctx") * tokens).astype(jnp.int32).reshape(1)
    ids = expert_ids[0].T
    logits = router_logits[0].T

    copies = jnp.broadcast_to(prompt_latent[None], (ctx_count,) + prompt_latent.shape)
    prompt = lax.all_to_all(copies, "ctx", 0, 0, tiled=True).reshape(-1, width)

    sent, slot = build_send(lengths, chosen, start, log_ratio, ids, logits, moe_cot[0])
    arrived = lax.all_to_all(
        unflat(sent, devices, per_owner, CAP, model), ("ctx", "resp"), 0, 0, tiled=True
    )

    grad_query, key_send = attention(
        lengths, chosen, log_ratio, queries[0], attn_cot[0], prompt, response_latent[0].T, ctx_count
    )
    key_rows = lax.all_to_all(key_send, "ctx", 0, 0, tiled=True).astype(f32).sum(axis=0)
    prompt_rows = prompt_latent.shape[0]
    grad_response = key_rows[prompt_rows:][None]
    prompt_part = key_rows[:prompt_rows].reshape(resp_count, prompt_rows // resp_count, width)
    grad_prompt = lax.all_to_all(prompt_part, "resp", 0, 0, tiled=True).sum(axis=0)

    dots = slot_dots(flat(arrived), flat(expert_outputs), model // LANES)
    dots = dots.reshape(devices, per_owner, 4, CAP).sum(axis=2)
    returned = lax.all_to_all(dots, ("ctx", "resp"), 0, 0, tiled=True)

    affinity, total, gate = router_gates(logits)
    gate_low = gate.astype(bf16).astype(f32)
    placing = (ids * CAP + slot).reshape(-1)
    gate_grad = jnp.take(returned.reshape(-1), placing).reshape(ids.shape) / gate_low
    mixed = jnp.sum(gate_grad * affinity, axis=0, keepdims=True) / total
    grad_router = route_scale / total * (gate_grad - mixed) * affinity * (1.0 - affinity)
    return (grad_query[None], grad_prompt, grad_response, arrived, grad_router.T[None])


def solution(mesh):
    placed = (
        P("resp", None, "ctx"),
        P("resp", None, "ctx"),
        P("ctx", None),
        P("resp", None, None),
        P("resp", None),
        P("resp", None),
        P("resp"),
        P("resp", "ctx", None),
        P("resp", "ctx", None),
        P("resp", "ctx", None),
        P(None, ("ctx", "resp"), None, None),
    )
    return jax.shard_map(
        on_device,
        mesh=mesh,
        in_specs=placed,
        out_specs=(
            P("resp", None, "ctx"),
            P(("ctx", "resp"), None),
            P("resp", "ctx", None),
            P(None, ("ctx", "resp"), None, None),
            P("resp", "ctx", None),
        ),
        check_vma=False,
    )
```

```python
import jax
import jax.numpy as jnp
from jax import lax
from jax.experimental import pallas as pl
from jax.experimental.pallas import tpu as pltpu
from jax.sharding import PartitionSpec as P

EXPERTS = 256
CAP = 2
LANES = 128
PLACED = 4
VMEM = 58 << 20

score_scale = 192.0 ** (-0.5)
preference_beta = 0.5
route_scale = 2.5
log2_e = 1.4426950408889634

f32 = jnp.float32
bf16 = jnp.bfloat16


def coefficient_row(ratio_ref, lengths_ref, chosen_ref):
    rows = ratio_ref.shape[1]
    half = rows // 2
    lane = lax.broadcasted_iota(jnp.int32, (1, rows), 1)
    second = lane >= half
    position = jnp.where(second, lane - half, lane)
    length = jnp.where(second, lengths_ref[0, 1], lengths_ref[0, 0])
    live = position < length
    ratios = jnp.where(live, ratio_ref[...], 0.0)
    first_total = jnp.sum(jnp.where(second, 0.0, ratios), axis=1, keepdims=True)
    second_total = jnp.sum(jnp.where(second, ratios, 0.0), axis=1, keepdims=True)
    chosen = chosen_ref[0]
    margin = first_total - second_total
    margin = jnp.where(chosen == 0, margin, -margin)
    weight = preference_beta * jax.nn.sigmoid(-preference_beta * margin)
    signed = jnp.where(second == (chosen == 1), -weight, weight)
    return jnp.where(live, signed, 0.0)


def column_of(row):
    n = row.shape[1]
    return jnp.transpose(jnp.broadcast_to(row, (8, n)))[:, :1]


def router_gates(logits):
    affinity = jax.nn.sigmoid(logits)
    total = jnp.sum(affinity, axis=0, keepdims=True)
    return affinity, total, route_scale * affinity / total


def send_kernel(
    lengths_ref, chosen_ref, start_ref, ratio_ref, ids_ref, logits_ref, cot_ref,
    send_hbm, slot_ref, rows_ref, pair_ref, table_ref, gates_ref, table_smem, gates_smem, send_ref,
    sems, send_sems,
):
    tokens, model = cot_ref.shape
    top = ids_ref.shape[0]
    tiles = model // LANES
    parts = send_sems.shape[0]
    per_part = EXPERTS // parts
    part_rows = per_part * tiles * CAP

    _, _, gate = router_gates(logits_ref[...])
    gate = gate.astype(bf16).astype(f32)
    ids = jnp.transpose(ids_ref[...])
    gates = jnp.transpose(gate)
    expert = lax.broadcasted_iota(jnp.int32, (tokens, EXPERTS), 1)
    named = jnp.zeros((tokens, EXPERTS), f32)
    weight = jnp.zeros((tokens, EXPERTS), f32)
    for n in range(top):
        hit = ids[:, n : n + 1] == expert
        named = jnp.where(hit, 1.0, named)
        weight = jnp.where(hit, gates[:, n : n + 1], weight)
    row_i = lax.broadcasted_iota(jnp.int32, (tokens, tokens), 0)
    col_i = lax.broadcasted_iota(jnp.int32, (tokens, tokens), 1)
    before = jnp.dot(
        (col_i < row_i).astype(bf16), named.astype(bf16), preferred_element_type=f32
    )
    token = lax.broadcasted_iota(jnp.int32, (tokens, EXPERTS), 0).astype(f32)
    for s in range(CAP):
        here = jnp.where((before == float(s)) & (named > 0.0), 1.0, 0.0)
        table_ref[s : s + 1, :] = jnp.sum(here * token, axis=0, keepdims=True).astype(jnp.int32)
        gates_ref[s : s + 1, :] = jnp.sum(here * weight, axis=0, keepdims=True)
    table_copy = pltpu.make_async_copy(table_ref, table_smem, sems.at[0])
    gates_copy = pltpu.make_async_copy(gates_ref, gates_smem, sems.at[1])
    table_copy.start()
    gates_copy.start()
    slots = []
    for n in range(top):
        hit = ids[:, n : n + 1] == expert
        slots.append(jnp.sum(jnp.where(hit, before, 0.0), axis=1, keepdims=True))
    slot_ref[...] = jnp.transpose(jnp.concatenate(slots, axis=1)).astype(jnp.int32)
    coefficient = coefficient_row(ratio_ref, lengths_ref, chosen_ref)
    lane = lax.broadcasted_iota(jnp.int32, (tokens, coefficient.shape[1]), 1)
    row = lax.broadcasted_iota(jnp.int32, (tokens, coefficient.shape[1]), 0)
    own = jnp.sum(
        jnp.where(lane == row + start_ref[0], coefficient, 0.0), axis=1, keepdims=True
    )
    for tile in range(tiles):
        cot = cot_ref[:, tile * LANES : (tile + 1) * LANES].astype(f32)
        rows_ref[pl.ds(tile, tokens, stride=tiles), :] = (own * cot).astype(bf16).astype(f32)
    table_copy.wait()
    gates_copy.wait()

    def place(group, carry):
        for u in range(PLACED):
            e = group * PLACED + u
            for s in range(CAP):
                token = table_smem[s, e]
                block = rows_ref[pl.ds(pl.multiple_of(token * tiles, 8), tiles), :]
                pair_ref[u, pl.ds(s, tiles, stride=CAP), :] = block * gates_smem[s, e]
        for u in range(PLACED):
            at = pl.multiple_of((group * PLACED + u) * (tiles * CAP), 16)
            send_ref[pl.ds(at, tiles * CAP), :] = pair_ref[u].astype(bf16)
        return carry

    def send_copy(part):
        at = pl.ds(pl.multiple_of(part * part_rows, 16), part_rows)
        return pltpu.make_async_copy(send_ref.at[at], send_hbm.at[at], send_sems.at[part])

    def one_part(part, carry):
        first = part * (per_part // PLACED)
        lax.fori_loop(0, per_part // PLACED, lambda g, c: place(first + g, c), 0, unroll=2)
        send_copy(part).start()
        return carry

    lax.fori_loop(0, parts, one_part, 0)
    for part in range(parts):
        send_copy(part).wait()


def build_send(lengths, chosen, start, ratio, ids, logits, cot):
    tokens, model = cot.shape
    tiles = model // LANES
    rows = EXPERTS * CAP * tiles
    parts = 8
    smem = pl.BlockSpec(memory_space=pltpu.SMEM)
    vmem = pl.BlockSpec(memory_space=pltpu.VMEM)
    return pl.pallas_call(
        send_kernel,
        in_specs=[smem, smem, smem, vmem, vmem, vmem, vmem],
        out_specs=[pl.BlockSpec(memory_space=pl.ANY), vmem],
        out_shape=[
            jax.ShapeDtypeStruct((rows, LANES), bf16),
            jax.ShapeDtypeStruct(ids.shape, jnp.int32),
        ],
        scratch_shapes=[
            pltpu.VMEM((tokens * tiles, LANES), f32),
            pltpu.VMEM((PLACED, tiles * CAP, LANES), f32),
            pltpu.VMEM((8, EXPERTS), jnp.int32),
            pltpu.VMEM((8, EXPERTS), f32),
            pltpu.SMEM((8, EXPERTS), jnp.int32),
            pltpu.SMEM((8, EXPERTS), f32),
            pltpu.VMEM((rows, LANES), bf16),
            pltpu.SemaphoreType.DMA((2,)),
            pltpu.SemaphoreType.DMA((parts,)),
        ],
        compiler_params=pltpu.CompilerParams(vmem_limit_bytes=VMEM),
        cost_estimate=pl.CostEstimate(flops=0, bytes_accessed=8_000_000, transcendentals=0),
        name="build_send",
    )(lengths, chosen, start, ratio, ids, logits, cot)


def dot_kernel(got_hbm, saved_hbm, out_ref, rows_hbm, got_ref, saved_ref, acc_ref, sems):
    sources, wide = out_ref.shape
    per_owner = wide // 8
    parts = sems.shape[1]
    rows = got_ref.shape[0] // parts
    owners = sources // parts
    tall = rows // (owners * per_owner)

    def copies(part):
        at = pl.ds(pl.multiple_of(part * rows, 16), rows)
        return (
            pltpu.make_async_copy(got_hbm.at[at], got_ref.at[at], sems.at[0, part]),
            pltpu.make_async_copy(saved_hbm.at[at], saved_ref.at[at], sems.at[1, part]),
        )

    def pass_on(part):
        at = pl.ds(pl.multiple_of(part * rows, 16), rows)
        return pltpu.make_async_copy(got_ref.at[at], rows_hbm.at[at], sems.at[2, part])

    for part in range(parts):
        for copy in copies(part):
            copy.start()

    def work(part, carry):
        for copy in copies(part):
            copy.wait()
        pass_on(part).start()
        for p in range(owners * per_owner):
            at = pl.ds(pl.multiple_of(part * rows + p * tall, 16), tall)
            product = got_ref[at, :].astype(f32) * saved_ref[at, :].astype(f32)
            acc_ref[p] = jnp.sum(product.reshape(tall // 8, 8, LANES), axis=0)
        product = acc_ref[...].reshape(owners, per_owner, 8, LANES)
        out_ref[pl.ds(pl.multiple_of(part * owners, 8), owners), :] = jnp.concatenate(
            [jnp.sum(product[:, e], axis=2) for e in range(per_owner)], axis=1
        )
        return carry

    lax.fori_loop(0, parts, work, 0)
    for part in range(parts):
        pass_on(part).wait()


def slot_dots(got, saved, sources, per_owner):
    parts = 8
    anywhere = pl.BlockSpec(memory_space=pl.ANY)
    return pl.pallas_call(
        dot_kernel,
        in_specs=[anywhere, anywhere],
        out_specs=[pl.BlockSpec(memory_space=pltpu.VMEM), anywhere],
        out_shape=[
            jax.ShapeDtypeStruct((sources, per_owner * 8), f32),
            jax.ShapeDtypeStruct(got.shape, got.dtype),
        ],
        scratch_shapes=[
            pltpu.VMEM(got.shape, got.dtype),
            pltpu.VMEM(got.shape, got.dtype),
            pltpu.VMEM((sources // parts * per_owner, 8, LANES), f32),
            pltpu.SemaphoreType.DMA((3, parts)),
        ],
        compiler_params=pltpu.CompilerParams(vmem_limit_bytes=VMEM),
        cost_estimate=pl.CostEstimate(flops=8_000_000, bytes_accessed=15_000_000, transcendentals=0),
        name="slot_dots",
    )(got, saved)


def router_kernel(terms_ref, ids_ref, slot_ref, logits_ref, out_ref):
    top, tokens = ids_ref.shape
    owners, wide = terms_ref.shape
    per_owner = wide // 8
    affinity, total, gate = router_gates(logits_ref[...])
    ids = jnp.transpose(ids_ref[...])
    slots = jnp.transpose(slot_ref[...])
    terms = jnp.transpose(terms_ref[...])
    owner = lax.broadcasted_iota(jnp.int32, (tokens, owners), 1)
    columns = []
    for n in range(top):
        expert = ids[:, n : n + 1]
        slot = slots[:, n : n + 1]
        picked = jnp.zeros((tokens, owners), f32)
        for e in range(per_owner):
            for s in range(CAP):
                dot = jnp.zeros((1, owners), f32)
                for k in range(s, 8, CAP):
                    dot = dot + terms[e * 8 + k : e * 8 + k + 1]
                hit = (owner * per_owner + e == expert) & (slot == s)
                picked = jnp.where(hit, dot, picked)
        columns.append(jnp.sum(picked, axis=1, keepdims=True))
    gate_grad = jnp.transpose(jnp.concatenate(columns, axis=1)) / gate.astype(bf16).astype(f32)
    mixed = jnp.sum(gate_grad * affinity, axis=0, keepdims=True) / total
    out_ref[...] = route_scale / total * (gate_grad - mixed) * affinity * (1.0 - affinity)


def router_grad(terms, ids, slot, logits):
    return pl.pallas_call(
        router_kernel,
        out_shape=jax.ShapeDtypeStruct(logits.shape, f32),
        compiler_params=pltpu.CompilerParams(vmem_limit_bytes=VMEM),
        name="router_grad",
    )(terms, ids, slot, logits)


NT = (((1,), (1,)), ((), ()))


def attention_kernel(
    lengths_ref, chosen_ref, place_ref, ratio_ref, q_ref, cot_ref, prompt_ref, answer_ref,
    gq_ref, keep_ref, send_ref, keys_ref, keys_t_ref, acc_ref, value_ref,
):
    prompt_count, width = prompt_ref.shape
    row_count = answer_ref.shape[1]
    half = row_count // 2
    wide = keys_ref.shape[2]
    rank = value_ref.shape[1]
    pad = wide - width
    step = pl.program_id(0)

    @pl.when(step == 0)
    def _():
        answer_t = answer_ref[...]
        keys_t_ref[:, :prompt_count] = jnp.transpose(prompt_ref[...])
        keys_t_ref[:, prompt_count:] = answer_t
        latent = jnp.concatenate([prompt_ref[...], jnp.transpose(answer_t)], axis=0)
        zeros = jnp.zeros((latent.shape[0], pad), bf16)
        keys_ref[0] = jnp.concatenate([latent, zeros], axis=1)
        keys_ref[1] = jnp.concatenate([zeros, latent], axis=1)
        acc_ref[...] = jnp.zeros_like(acc_ref)
        value_ref[...] = jnp.zeros_like(value_ref)

    coefficient = column_of(coefficient_row(ratio_ref, lengths_ref, chosen_ref))
    key_i = lax.broadcasted_iota(jnp.int32, (half, half), 0)
    row_i = lax.broadcasted_iota(jnp.int32, (half, half), 1)
    causal = key_i <= row_i
    for k in range(2):
        rows = slice(k * half, (k + 1) * half)
        answer = slice(prompt_count + k * half, prompt_count + (k + 1) * half)
        grads = []
        for h in range(2):
            query = q_ref[rows, h * rank : h * rank + wide]
            grad_out = (
                coefficient[rows] * cot_ref[rows, h * rank : (h + 1) * rank].astype(f32)
            ).astype(bf16)
            s_prompt = lax.dot_general(
                keys_ref[h, :prompt_count], query, NT, preferred_element_type=f32
            )
            s_answer = lax.dot_general(keys_ref[h, answer], query, NT, preferred_element_type=f32)
            s_answer = jnp.where(causal, s_answer, -1e30)
            top = jnp.maximum(
                jnp.max(s_prompt, axis=0, keepdims=True), jnp.max(s_answer, axis=0, keepdims=True)
            )
            e_prompt = jnp.exp2((s_prompt - top) * (score_scale * log2_e))
            e_answer = jnp.exp2((s_answer - top) * (score_scale * log2_e))
            total = jnp.sum(e_prompt, axis=0, keepdims=True) + jnp.sum(
                e_answer, axis=0, keepdims=True
            )
            inverse = 1.0 / total
            p_prompt = e_prompt * inverse
            p_answer = e_answer * inverse
            b_prompt = p_prompt.astype(bf16)
            b_answer = p_answer.astype(bf16)
            d_prompt = lax.dot_general(
                keys_ref[0, :prompt_count, :rank], grad_out, NT, preferred_element_type=f32
            )
            d_answer = lax.dot_general(
                keys_ref[0, answer, :rank], grad_out, NT, preferred_element_type=f32
            )
            delta = jnp.sum(b_prompt.astype(f32) * d_prompt, axis=0, keepdims=True) + jnp.sum(
                b_answer.astype(f32) * d_answer, axis=0, keepdims=True
            )
            g_prompt = (p_prompt * (d_prompt - delta)).astype(bf16)
            g_answer = (p_answer * (d_answer - delta)).astype(bf16)
            grads.append(
                jnp.dot(keys_t_ref[:, :prompt_count], g_prompt, preferred_element_type=f32)
                + jnp.dot(keys_t_ref[:, answer], g_answer, preferred_element_type=f32)
            )
            acc_ref[h, :prompt_count] += jnp.dot(g_prompt, query, preferred_element_type=f32)
            acc_ref[h, answer] += jnp.dot(g_answer, query, preferred_element_type=f32)
            value_ref[:prompt_count] += jnp.dot(b_prompt, grad_out, preferred_element_type=f32)
            value_ref[answer] += jnp.dot(b_answer, grad_out, preferred_element_type=f32)
        both = (score_scale * jnp.concatenate(grads, axis=0)).astype(bf16)
        gq_ref[rows, :] = jnp.transpose(both)

    @pl.when(step == pl.num_programs(0) - 1)
    def _():
        half_chunks = send_ref.shape[0]
        prompt_rows = prompt_count // (2 * half_chunks)
        answer_rows = row_count // (2 * half_chunks)

        def combined(at):
            size = at.size
            key = acc_ref[0, at, :width] + pltpu.roll(acc_ref[1, at, :], wide - pad, 1)[:, :width]
            value = jnp.concatenate([value_ref[at, :], jnp.zeros((size, width - rank), f32)], axis=1)
            return (score_scale * key + value).astype(bf16)

        for side, out in enumerate((keep_ref, send_ref)):
            for c in range(half_chunks):
                chunk = side * half_chunks + c
                out[c, :prompt_rows] = combined(pl.ds(chunk * prompt_rows, prompt_rows))
                at = pl.multiple_of(prompt_count + place_ref[chunk] * answer_rows, answer_rows)
                out[c, prompt_rows:] = combined(pl.ds(at, answer_rows))


def attention(lengths, chosen, place, ratio, queries, cot, prompt, answer_t):
    rows, q_width = queries.shape
    prompt_count, width = prompt.shape
    heads = q_width // width
    rank = cot.shape[1] // heads
    wide = width + width - rank
    steps = heads // 2
    keys = prompt_count + rows
    chunks = place.shape[0]
    part = (chunks // 2, keys // chunks, width)
    whole = lambda shape: pl.BlockSpec(shape, lambda i: (0,) * len(shape))
    smem = pl.BlockSpec(memory_space=pltpu.SMEM)
    return pl.pallas_call(
        attention_kernel,
        grid=(steps,),
        in_specs=[
            smem, smem, smem, whole(ratio.shape),
            pl.BlockSpec((rows, 2 * width), lambda i: (0, i)),
            pl.BlockSpec((rows, 2 * rank), lambda i: (0, i)),
            whole(prompt.shape), whole(answer_t.shape),
        ],
        out_specs=[
            pl.BlockSpec((rows, 2 * width), lambda i: (0, i)),
            whole(part),
            whole(part),
        ],
        out_shape=[
            jax.ShapeDtypeStruct(queries.shape, bf16),
            jax.ShapeDtypeStruct(part, bf16),
            jax.ShapeDtypeStruct(part, bf16),
        ],
        scratch_shapes=[
            pltpu.VMEM((2, keys, wide), bf16),
            pltpu.VMEM((width, keys), bf16),
            pltpu.VMEM((2, keys, wide), f32),
            pltpu.VMEM((keys, rank), f32),
        ],
        compiler_params=pltpu.CompilerParams(vmem_limit_bytes=VMEM),
        cost_estimate=pl.CostEstimate(
            flops=17_000_000_000, bytes_accessed=9_000_000, transcendentals=2_600_000
        ),
        name="attention",
    )(lengths, chosen, place, ratio, queries, cot, prompt, answer_t)


def flat(x):
    n, e, s, d = x.shape
    t = d // LANES
    return x.reshape(n, e, s, t, LANES).transpose(0, 1, 3, 2, 4).reshape(n * e * t * s, LANES)


def unflat(x, n, e, s, d):
    t = d // LANES
    return x.reshape(n, e, t, s, LANES).transpose(0, 1, 3, 2, 4).reshape(n, e, s, d)


def ctx_moves(count, far, ring, core):
    rings = count // 4
    moves = []
    for f in range(2):
        for r in range(rings):
            for c in range(2):
                source = (f * rings + r) * 2 + c
                moves.append((source, ((f ^ far) * rings + (r + ring) % rings) * 2 + (c ^ core)))
    return moves


def resp_moves(count, ring, far):
    rings = count // 2
    return [
        (r * 2 + f, (r + ring) % rings * 2 + (f ^ far)) for r in range(rings) for f in range(2)
    ]


def gather_ring(latent, count):
    rings = count // 4
    return jnp.concatenate(
        [latent]
        + [lax.ppermute(latent, "ctx", ctx_moves(count, 0, rings - d, 0)) for d in range(1, rings)]
    )


def ctx_places(count):
    rings = count // 4
    me = lax.axis_index("ctx")
    order = jnp.arange(count, dtype=jnp.int32)
    core, far, ring = order // (rings * 2), order // rings % 2, order % rings
    my_core, my_ring, my_far = me % 2, me // 2 % rings, me // (rings * 2)
    return ((my_far ^ far) * rings + (my_ring + ring) % rings) * 2 + (my_core ^ core)


def reduce_over_cores(keep, send, count):
    got = lax.ppermute(send, "ctx", ctx_moves(count, 0, 0, 1))
    return (keep.astype(f32) + got.astype(f32)).reshape((2, count // 4) + keep.shape[1:])


def both_moves(ctx_count, resp_count):
    return [
        (c0 * resp_count + r0, c1 * resp_count + r1)
        for c0, c1 in ctx_moves(ctx_count, 1, 0, 0)
        for r0, r1 in resp_moves(resp_count, 0, 1)
    ]


def reduce_over_ring(held, count):
    low = held.astype(bf16)
    mine = held[:, 0]
    for d in range(1, count // 4):
        mine = mine + lax.ppermute(low[:, d], "ctx", ctx_moves(count, 0, d, 0)).astype(f32)
    return mine


def reduce_answer(rows, count):
    return rows[0] + lax.ppermute(rows[1], "ctx", ctx_moves(count, 1, 0, 0))


def reduce_prompt(rows, ctx_count, resp_count):
    rings = resp_count // 2
    me = lax.axis_index("resp")
    my_ring, my_far = me // 2, me % 2
    blocks = rows.reshape(2, rings, 2, rows.shape[1] // resp_count, rows.shape[2])
    twice = jnp.concatenate([blocks, blocks[:, : rings - 1]], axis=1)
    blocks = lax.dynamic_slice_in_dim(twice, my_ring, rings, axis=1)
    mine = blocks[:, 0]
    for d in range(1, rings):
        mine = mine + lax.ppermute(blocks[:, d], "resp", resp_moves(resp_count, d, 0))
    own = lax.dynamic_index_in_dim(mine, my_far, axis=1, keepdims=False)
    others = lax.dynamic_index_in_dim(mine, 1 - my_far, axis=1, keepdims=False)
    return (
        own[0]
        + lax.ppermute(own[1], "ctx", ctx_moves(ctx_count, 1, 0, 0))
        + lax.ppermute(others[0], "resp", resp_moves(resp_count, 0, 1))
        + lax.ppermute(others[1], ("ctx", "resp"), both_moves(ctx_count, resp_count))
    )


def on_device(
    queries,
    attn_cot,
    prompt_latent,
    response_latent,
    log_ratio,
    lengths,
    chosen,
    moe_cot,
    expert_ids,
    router_logits,
    expert_outputs,
):
    ctx_count = lax.axis_size("ctx")
    resp_count = lax.axis_size("resp")
    devices = ctx_count * resp_count
    width = prompt_latent.shape[1]
    tokens, model = moe_cot.shape[1:]
    per_owner = EXPERTS // devices
    start = (lax.axis_index("ctx") * tokens).astype(jnp.int32).reshape(1)
    ids = expert_ids[0].T
    logits = router_logits[0].T

    ring = gather_ring(prompt_latent, ctx_count)
    ring, cot = lax.optimization_barrier((ring, moe_cot[0]))
    sent, slot = build_send(lengths, chosen, start, log_ratio, ids, logits, cot)
    far = lax.ppermute(ring, "ctx", ctx_moves(ctx_count, 1, 0, 0))
    sent, around = lax.optimization_barrier((sent, jnp.concatenate([ring, far])))
    other = lax.ppermute(around, "ctx", ctx_moves(ctx_count, 0, 0, 1))
    arrived = lax.all_to_all(
        unflat(sent, devices, per_owner, CAP, model), ("ctx", "resp"), 0, 0, tiled=True
    )

    grad_query, keep, send = attention(
        lengths, chosen, ctx_places(ctx_count), log_ratio, queries[0], attn_cot[0],
        jnp.concatenate([around, other]), response_latent[0].T,
    )
    held = reduce_over_cores(keep, send, ctx_count)
    terms, rows = slot_dots(flat(arrived), flat(expert_outputs), devices, per_owner)
    mine = reduce_over_ring(held, ctx_count)
    mine, terms = lax.optimization_barrier((mine, terms))
    returned = lax.all_to_all(terms, ("ctx", "resp"), 0, 0, tiled=True)
    prompt_rows = prompt_latent.shape[0]
    grad_response = reduce_answer(mine[:, prompt_rows:], ctx_count)[None]
    grad_prompt = reduce_prompt(mine[:, :prompt_rows], ctx_count, resp_count)

    returned, grad_prompt, grad_response = lax.optimization_barrier(
        (returned, grad_prompt, grad_response)
    )
    grad_router = router_grad(returned, ids, slot, logits)
    expert_row_grads = unflat(rows, devices, per_owner, CAP, model)
    return (grad_query[None], grad_prompt, grad_response, expert_row_grads, grad_router.T[None])


def solution(mesh):
    placed = (
        P("resp", None, "ctx"),
        P("resp", None, "ctx"),
        P("ctx", None),
        P("resp", None, None),
        P("resp", None),
        P("resp", None),
        P("resp"),
        P("resp", "ctx", None),
        P("resp", "ctx", None),
        P("resp", "ctx", None),
        P(None, ("ctx", "resp"), None, None),
    )
    return jax.shard_map(
        on_device,
        mesh=mesh,
        in_specs=placed,
        out_specs=(
            P("resp", None, "ctx"),
            P(("ctx", "resp"), None),
            P("resp", "ctx", None),
            P(None, ("ctx", "resp"), None, None),
            P("resp", "ctx", None),
        ),
        check_vma=False,
    )
```

```python
import jax
import jax.numpy as jnp
from jax import lax
from jax.experimental import pallas as pl
from jax.experimental.pallas import tpu as pltpu
from jax.sharding import PartitionSpec as P

EXPERTS = 256
CAP = 2
LANES = 128
PLACED = 4
VMEM = 58 << 20

score_scale = 192.0 ** (-0.5)
preference_beta = 0.5
route_scale = 2.5
log2_e = 1.4426950408889634

f32 = jnp.float32
bf16 = jnp.bfloat16


def coefficient_row(ratio_ref, lengths_ref, chosen_ref):
    rows = ratio_ref.shape[1]
    half = rows // 2
    lane = lax.broadcasted_iota(jnp.int32, (1, rows), 1)
    second = lane >= half
    position = jnp.where(second, lane - half, lane)
    length = jnp.where(second, lengths_ref[0, 1], lengths_ref[0, 0])
    live = position < length
    ratios = jnp.where(live, ratio_ref[...], 0.0)
    first_total = jnp.sum(jnp.where(second, 0.0, ratios), axis=1, keepdims=True)
    second_total = jnp.sum(jnp.where(second, ratios, 0.0), axis=1, keepdims=True)
    chosen = chosen_ref[0]
    margin = first_total - second_total
    margin = jnp.where(chosen == 0, margin, -margin)
    weight = preference_beta * jax.nn.sigmoid(-preference_beta * margin)
    signed = jnp.where(second == (chosen == 1), -weight, weight)
    return jnp.where(live, signed, 0.0)


def column_of(row):
    n = row.shape[1]
    return jnp.transpose(jnp.broadcast_to(row, (8, n)))[:, :1]


def router_gates(logits):
    affinity = jax.nn.sigmoid(logits)
    total = jnp.sum(affinity, axis=0, keepdims=True)
    return affinity, total, route_scale * affinity / total


def plan_kernel(
    lengths_ref, chosen_ref, start_ref, ratio_ref, ids_ref, logits_ref, cot_ref,
    rows_ref, slot_ref, table_ref, gates_ref,
):
    tokens, model = cot_ref.shape
    top = ids_ref.shape[0]
    tiles = model // LANES
    _, _, gate = router_gates(logits_ref[...])
    gate = gate.astype(bf16).astype(f32)
    ids = jnp.transpose(ids_ref[...])
    gates = jnp.transpose(gate)
    expert = lax.broadcasted_iota(jnp.int32, (tokens, EXPERTS), 1)
    named = jnp.zeros((tokens, EXPERTS), f32)
    weight = jnp.zeros((tokens, EXPERTS), f32)
    for n in range(top):
        hit = ids[:, n : n + 1] == expert
        named = jnp.where(hit, 1.0, named)
        weight = jnp.where(hit, gates[:, n : n + 1], weight)
    row_i = lax.broadcasted_iota(jnp.int32, (tokens, tokens), 0)
    col_i = lax.broadcasted_iota(jnp.int32, (tokens, tokens), 1)
    before = jnp.dot((col_i < row_i).astype(bf16), named.astype(bf16), preferred_element_type=f32)
    token = lax.broadcasted_iota(jnp.int32, (tokens, EXPERTS), 0).astype(f32)
    for s in range(CAP):
        here = jnp.where((before == float(s)) & (named > 0.0), 1.0, 0.0)
        table_ref[s : s + 1, :] = jnp.sum(here * token, axis=0, keepdims=True).astype(jnp.int32)
        gates_ref[s : s + 1, :] = jnp.sum(here * weight, axis=0, keepdims=True)
    slots = []
    for n in range(top):
        hit = ids[:, n : n + 1] == expert
        slots.append(jnp.sum(jnp.where(hit, before, 0.0), axis=1, keepdims=True))
    slot_ref[...] = jnp.transpose(jnp.concatenate(slots, axis=1)).astype(jnp.int32)
    coefficient = coefficient_row(ratio_ref, lengths_ref, chosen_ref)
    lane = lax.broadcasted_iota(jnp.int32, (tokens, coefficient.shape[1]), 1)
    row = lax.broadcasted_iota(jnp.int32, (tokens, coefficient.shape[1]), 0)
    own = jnp.sum(jnp.where(lane == row + start_ref[0], coefficient, 0.0), axis=1, keepdims=True)
    for tile in range(tiles):
        cot = cot_ref[:, tile * LANES : (tile + 1) * LANES].astype(f32)
        rows_ref[pl.ds(tile, tokens, stride=tiles), :] = (own * cot).astype(bf16).astype(f32)


def plan_send(lengths, chosen, start, ratio, ids, logits, cot):
    tokens, model = cot.shape
    smem = pl.BlockSpec(memory_space=pltpu.SMEM)
    vmem = pl.BlockSpec(memory_space=pltpu.VMEM)
    return pl.pallas_call(
        plan_kernel,
        in_specs=[smem, smem, smem, vmem, vmem, vmem, vmem],
        out_specs=[vmem, vmem, vmem, vmem],
        out_shape=[
            jax.ShapeDtypeStruct((tokens * (model // LANES), LANES), f32),
            jax.ShapeDtypeStruct(ids.shape, jnp.int32),
            jax.ShapeDtypeStruct((CAP, EXPERTS), jnp.int32),
            jax.ShapeDtypeStruct((CAP, EXPERTS), f32),
        ],
        compiler_params=pltpu.CompilerParams(vmem_limit_bytes=VMEM),
        cost_estimate=pl.CostEstimate(flops=0, bytes_accessed=1_500_000, transcendentals=0),
        name="plan_send",
    )(lengths, chosen, start, ratio, ids, logits, cot)


def send_kernel(table_ref, gates_ref, rows_ref, send_hbm, pair_ref, send_ref, send_sems):
    tiles = pair_ref.shape[1] // CAP
    parts = send_sems.shape[0]
    per_part = EXPERTS // parts
    part_rows = per_part * tiles * CAP

    def place(group, carry):
        for u in range(PLACED):
            e = group * PLACED + u
            for s in range(CAP):
                token = table_ref[s, e]
                block = rows_ref[pl.ds(pl.multiple_of(token * tiles, 8), tiles), :]
                pair_ref[u, pl.ds(s, tiles, stride=CAP), :] = block * gates_ref[s, e]
        for u in range(PLACED):
            at = pl.multiple_of((group * PLACED + u) * (tiles * CAP), 16)
            send_ref[pl.ds(at, tiles * CAP), :] = pair_ref[u].astype(bf16)
        return carry

    def send_copy(part):
        at = pl.ds(pl.multiple_of(part * part_rows, 16), part_rows)
        return pltpu.make_async_copy(send_ref.at[at], send_hbm.at[at], send_sems.at[part])

    def one_part(part, carry):
        first = part * (per_part // PLACED)
        lax.fori_loop(0, per_part // PLACED, lambda g, c: place(first + g, c), 0, unroll=2)
        send_copy(part).start()
        return carry

    lax.fori_loop(0, parts, one_part, 0)
    for part in range(parts):
        send_copy(part).wait()


def build_send(table, gates, token_rows, tokens):
    tiles = token_rows.shape[0] // tokens
    rows = EXPERTS * CAP * tiles
    parts = 8
    smem = pl.BlockSpec(memory_space=pltpu.SMEM)
    vmem = pl.BlockSpec(memory_space=pltpu.VMEM)
    return pl.pallas_call(
        send_kernel,
        in_specs=[smem, smem, vmem],
        out_specs=pl.BlockSpec(memory_space=pl.ANY),
        out_shape=jax.ShapeDtypeStruct((rows, LANES), bf16),
        scratch_shapes=[
            pltpu.VMEM((PLACED, tiles * CAP, LANES), f32),
            pltpu.VMEM((rows, LANES), bf16),
            pltpu.SemaphoreType.DMA((parts,)),
        ],
        compiler_params=pltpu.CompilerParams(vmem_limit_bytes=VMEM),
        cost_estimate=pl.CostEstimate(flops=0, bytes_accessed=8_000_000, transcendentals=0),
        name="build_send",
    )(table, gates, token_rows)


def dot_kernel(got_hbm, saved_hbm, out_ref, rows_hbm, got_ref, saved_ref, acc_ref, sems):
    sources = out_ref.shape[0]
    per_owner = EXPERTS // sources
    parts = sems.shape[1]
    rows = got_ref.shape[0] // parts
    owners = sources // parts
    tall = rows // (owners * per_owner)

    def copies(part):
        at = pl.ds(pl.multiple_of(part * rows, 16), rows)
        return (
            pltpu.make_async_copy(got_hbm.at[at], got_ref.at[at], sems.at[0, part]),
            pltpu.make_async_copy(saved_hbm.at[at], saved_ref.at[at], sems.at[1, part]),
        )

    def pass_on(part):
        at = pl.ds(pl.multiple_of(part * rows, 16), rows)
        return pltpu.make_async_copy(got_ref.at[at], rows_hbm.at[at], sems.at[2, part])

    for part in range(parts):
        for copy in copies(part):
            copy.start()

    def work(part, carry):
        for copy in copies(part):
            copy.wait()
        pass_on(part).start()
        for p in range(owners * per_owner):
            at = pl.ds(pl.multiple_of(part * rows + p * tall, 16), tall)
            product = got_ref[at, :].astype(f32) * saved_ref[at, :].astype(f32)
            acc_ref[p] = jnp.sum(product.reshape(tall // 8, 8, LANES), axis=0)
        product = acc_ref[...].reshape(owners, per_owner, 8, LANES)
        spare = jnp.zeros((owners, LANES - 8 * per_owner), f32)
        out_ref[pl.ds(pl.multiple_of(part * owners, 8), owners), :] = jnp.concatenate(
            [jnp.sum(product[:, e], axis=2) for e in range(per_owner)] + [spare], axis=1
        )
        return carry

    lax.fori_loop(0, parts, work, 0)
    for part in range(parts):
        pass_on(part).wait()


def slot_dots(got, saved, sources, per_owner):
    parts = 8
    anywhere = pl.BlockSpec(memory_space=pl.ANY)
    return pl.pallas_call(
        dot_kernel,
        in_specs=[anywhere, anywhere],
        out_specs=[pl.BlockSpec(memory_space=pltpu.VMEM), anywhere],
        out_shape=[
            jax.ShapeDtypeStruct((sources, LANES), f32),
            jax.ShapeDtypeStruct(got.shape, got.dtype),
        ],
        scratch_shapes=[
            pltpu.VMEM(got.shape, got.dtype),
            pltpu.VMEM(got.shape, got.dtype),
            pltpu.VMEM((sources // parts * per_owner, 8, LANES), f32),
            pltpu.SemaphoreType.DMA((3, parts)),
        ],
        compiler_params=pltpu.CompilerParams(vmem_limit_bytes=VMEM),
        cost_estimate=pl.CostEstimate(flops=8_000_000, bytes_accessed=15_000_000, transcendentals=0),
        name="slot_dots",
    )(got, saved)


def router_kernel(terms_ref, ids_ref, slot_ref, logits_ref, out_ref):
    top, tokens = ids_ref.shape
    owners = terms_ref.shape[0]
    per_owner = EXPERTS // owners
    affinity, total, gate = router_gates(logits_ref[...])
    ids = jnp.transpose(ids_ref[...])
    slots = jnp.transpose(slot_ref[...])
    terms = jnp.transpose(terms_ref[...])
    owner = lax.broadcasted_iota(jnp.int32, (tokens, owners), 1)
    columns = []
    for n in range(top):
        expert = ids[:, n : n + 1]
        slot = slots[:, n : n + 1]
        picked = jnp.zeros((tokens, owners), f32)
        for e in range(per_owner):
            for s in range(CAP):
                dot = jnp.zeros((1, owners), f32)
                for k in range(s, 8, CAP):
                    dot = dot + terms[e * 8 + k : e * 8 + k + 1]
                hit = (owner * per_owner + e == expert) & (slot == s)
                picked = jnp.where(hit, dot, picked)
        columns.append(jnp.sum(picked, axis=1, keepdims=True))
    gate_grad = jnp.transpose(jnp.concatenate(columns, axis=1)) / gate.astype(bf16).astype(f32)
    mixed = jnp.sum(gate_grad * affinity, axis=0, keepdims=True) / total
    out_ref[...] = route_scale / total * (gate_grad - mixed) * affinity * (1.0 - affinity)


def router_grad(terms, ids, slot, logits):
    return pl.pallas_call(
        router_kernel,
        out_shape=jax.ShapeDtypeStruct(logits.shape, f32),
        compiler_params=pltpu.CompilerParams(vmem_limit_bytes=VMEM),
        name="router_grad",
    )(terms, ids, slot, logits)


NT = (((1,), (1,)), ((), ()))


def attention_kernel(
    lengths_ref, chosen_ref, place_ref, ratio_ref, q_ref, cot_ref, prompt_ref, answer_ref,
    gq_ref, keep_ref, send_ref, keys_ref, keys_t_ref, acc_ref, value_ref,
):
    prompt_count, width = prompt_ref.shape
    row_count = answer_ref.shape[1]
    half = row_count // 2
    wide = keys_ref.shape[2]
    rank = value_ref.shape[1]
    pad = wide - width
    step = pl.program_id(0)

    @pl.when(step == 0)
    def _():
        answer_t = answer_ref[...]
        keys_t_ref[:, :prompt_count] = jnp.transpose(prompt_ref[...])
        keys_t_ref[:, prompt_count:] = answer_t
        latent = jnp.concatenate([prompt_ref[...], jnp.transpose(answer_t)], axis=0)
        zeros = jnp.zeros((latent.shape[0], pad), bf16)
        keys_ref[0] = jnp.concatenate([latent, zeros], axis=1)
        keys_ref[1] = jnp.concatenate([zeros, latent], axis=1)
        acc_ref[...] = jnp.zeros_like(acc_ref)
        value_ref[...] = jnp.zeros_like(value_ref)

    coefficient = column_of(coefficient_row(ratio_ref, lengths_ref, chosen_ref))
    key_i = lax.broadcasted_iota(jnp.int32, (half, half), 0)
    row_i = lax.broadcasted_iota(jnp.int32, (half, half), 1)
    causal = key_i <= row_i
    for k in range(2):
        rows = slice(k * half, (k + 1) * half)
        answer = slice(prompt_count + k * half, prompt_count + (k + 1) * half)
        grads = []
        for h in range(2):
            query = q_ref[rows, h * rank : h * rank + wide]
            grad_out = (
                coefficient[rows] * cot_ref[rows, h * rank : (h + 1) * rank].astype(f32)
            ).astype(bf16)
            s_prompt = lax.dot_general(
                keys_ref[h, :prompt_count], query, NT, preferred_element_type=f32
            )
            s_answer = lax.dot_general(keys_ref[h, answer], query, NT, preferred_element_type=f32)
            s_answer = jnp.where(causal, s_answer, -1e30)
            top = jnp.maximum(
                jnp.max(s_prompt, axis=0, keepdims=True), jnp.max(s_answer, axis=0, keepdims=True)
            )
            e_prompt = jnp.exp2((s_prompt - top) * (score_scale * log2_e))
            e_answer = jnp.exp2((s_answer - top) * (score_scale * log2_e))
            total = jnp.sum(e_prompt, axis=0, keepdims=True) + jnp.sum(
                e_answer, axis=0, keepdims=True
            )
            inverse = 1.0 / total
            p_prompt = e_prompt * inverse
            p_answer = e_answer * inverse
            b_prompt = p_prompt.astype(bf16)
            b_answer = p_answer.astype(bf16)
            d_prompt = lax.dot_general(
                keys_ref[0, :prompt_count, :rank], grad_out, NT, preferred_element_type=f32
            )
            d_answer = lax.dot_general(
                keys_ref[0, answer, :rank], grad_out, NT, preferred_element_type=f32
            )
            delta = jnp.sum(b_prompt.astype(f32) * d_prompt, axis=0, keepdims=True) + jnp.sum(
                b_answer.astype(f32) * d_answer, axis=0, keepdims=True
            )
            g_prompt = (p_prompt * (d_prompt - delta)).astype(bf16)
            g_answer = (p_answer * (d_answer - delta)).astype(bf16)
            grads.append(
                jnp.dot(keys_t_ref[:, :prompt_count], g_prompt, preferred_element_type=f32)
                + jnp.dot(keys_t_ref[:, answer], g_answer, preferred_element_type=f32)
            )
            acc_ref[h, :prompt_count] += jnp.dot(g_prompt, query, preferred_element_type=f32)
            acc_ref[h, answer] += jnp.dot(g_answer, query, preferred_element_type=f32)
            value_ref[:prompt_count] += jnp.dot(b_prompt, grad_out, preferred_element_type=f32)
            value_ref[answer] += jnp.dot(b_answer, grad_out, preferred_element_type=f32)
        both = (score_scale * jnp.concatenate(grads, axis=0)).astype(bf16)
        gq_ref[rows, :] = jnp.transpose(both)

    @pl.when(step == pl.num_programs(0) - 1)
    def _():
        half_chunks = send_ref.shape[0]
        prompt_rows = prompt_count // (2 * half_chunks)
        answer_rows = row_count // (2 * half_chunks)

        def combined(at):
            size = at.size
            key = acc_ref[0, at, :width] + pltpu.roll(acc_ref[1, at, :], wide - pad, 1)[:, :width]
            value = jnp.concatenate([value_ref[at, :], jnp.zeros((size, width - rank), f32)], axis=1)
            return (score_scale * key + value).astype(bf16)

        for side, out in enumerate((keep_ref, send_ref)):
            for c in range(half_chunks):
                chunk = side * half_chunks + c
                out[c, :prompt_rows] = combined(pl.ds(chunk * prompt_rows, prompt_rows))
                at = pl.multiple_of(prompt_count + place_ref[chunk] * answer_rows, answer_rows)
                out[c, prompt_rows:] = combined(pl.ds(at, answer_rows))


def attention(lengths, chosen, place, ratio, queries, cot, prompt, answer_t):
    rows, q_width = queries.shape
    prompt_count, width = prompt.shape
    heads = q_width // width
    rank = cot.shape[1] // heads
    wide = width + width - rank
    steps = heads // 2
    keys = prompt_count + rows
    chunks = place.shape[0]
    part = (chunks // 2, keys // chunks, width)
    whole = lambda shape: pl.BlockSpec(shape, lambda i: (0,) * len(shape))
    smem = pl.BlockSpec(memory_space=pltpu.SMEM)
    return pl.pallas_call(
        attention_kernel,
        grid=(steps,),
        in_specs=[
            smem, smem, smem, whole(ratio.shape),
            pl.BlockSpec((rows, 2 * width), lambda i: (0, i)),
            pl.BlockSpec((rows, 2 * rank), lambda i: (0, i)),
            whole(prompt.shape), whole(answer_t.shape),
        ],
        out_specs=[
            pl.BlockSpec((rows, 2 * width), lambda i: (0, i)),
            whole(part),
            whole(part),
        ],
        out_shape=[
            jax.ShapeDtypeStruct(queries.shape, bf16),
            jax.ShapeDtypeStruct(part, bf16),
            jax.ShapeDtypeStruct(part, bf16),
        ],
        scratch_shapes=[
            pltpu.VMEM((2, keys, wide), bf16),
            pltpu.VMEM((width, keys), bf16),
            pltpu.VMEM((2, keys, wide), f32),
            pltpu.VMEM((keys, rank), f32),
        ],
        compiler_params=pltpu.CompilerParams(vmem_limit_bytes=VMEM),
        cost_estimate=pl.CostEstimate(
            flops=17_000_000_000, bytes_accessed=9_000_000, transcendentals=2_600_000
        ),
        name="attention",
    )(lengths, chosen, place, ratio, queries, cot, prompt, answer_t)


def flat(x):
    n, e, s, d = x.shape
    t = d // LANES
    return x.reshape(n, e, s, t, LANES).transpose(0, 1, 3, 2, 4).reshape(n * e * t * s, LANES)


def unflat(x, n, e, s, d):
    t = d // LANES
    return x.reshape(n, e, t, s, LANES).transpose(0, 1, 3, 2, 4).reshape(n, e, s, d)


def ctx_moves(count, far, ring, core):
    rings = count // 4
    moves = []
    for f in range(2):
        for r in range(rings):
            for c in range(2):
                source = (f * rings + r) * 2 + c
                moves.append((source, ((f ^ far) * rings + (r + ring) % rings) * 2 + (c ^ core)))
    return moves


def resp_moves(count, ring, far):
    rings = count // 2
    return [
        (r * 2 + f, (r + ring) % rings * 2 + (f ^ far)) for r in range(rings) for f in range(2)
    ]


def gather_ring(rows, count):
    rings = count // 4
    return [lax.ppermute(rows, "ctx", ctx_moves(count, 0, rings - d, 0)) for d in range(1, rings)]


def ctx_places(count):
    rings = count // 4
    me = lax.axis_index("ctx")
    order = jnp.arange(count, dtype=jnp.int32)
    core, far, ring = order // (rings * 2), order // rings % 2, order % rings
    my_core, my_ring, my_far = me % 2, me // 2 % rings, me // (rings * 2)
    return ((my_far ^ far) * rings + (my_ring + ring) % rings) * 2 + (my_core ^ core)


def reduce_over_cores(keep, send, count):
    got = lax.ppermute(send, "ctx", ctx_moves(count, 0, 0, 1))
    return (keep.astype(f32) + got.astype(f32)).reshape((2, count // 4) + keep.shape[1:])


def both_moves(ctx_count, resp_count):
    return [
        (c0 * resp_count + r0, c1 * resp_count + r1)
        for c0, c1 in ctx_moves(ctx_count, 1, 0, 0)
        for r0, r1 in resp_moves(resp_count, 0, 1)
    ]


def ring_terms(held, count):
    low = held.astype(bf16)
    return [held[:, 0]] + [
        lax.ppermute(low[:, d], "ctx", ctx_moves(count, 0, d, 0)) for d in range(1, count // 4)
    ]


def reduce_answer(rows, count):
    return rows[0] + lax.ppermute(rows[1], "ctx", ctx_moves(count, 1, 0, 0))


def prompt_terms(rows, resp_count):
    rings = resp_count // 2
    me = lax.axis_index("resp")
    my_ring, my_far = me // 2, me % 2
    blocks = rows.reshape(2, rings, 2, rows.shape[1] // resp_count, rows.shape[2])
    twice = jnp.concatenate([blocks, blocks[:, : rings - 1]], axis=1)
    blocks = lax.dynamic_slice_in_dim(twice, my_ring, rings, axis=1)
    parts = [blocks[:, 0]] + [
        lax.ppermute(blocks[:, d], "resp", resp_moves(resp_count, d, 0)) for d in range(1, rings)
    ]
    return parts, my_far


def reduce_prompt_far(mine, my_far, ctx_count, resp_count):
    own = lax.dynamic_index_in_dim(mine, my_far, axis=1, keepdims=False)
    others = lax.dynamic_index_in_dim(mine, 1 - my_far, axis=1, keepdims=False)
    return (
        own[0]
        + lax.ppermute(own[1], "ctx", ctx_moves(ctx_count, 1, 0, 0))
        + lax.ppermute(others[0], "resp", resp_moves(resp_count, 0, 1))
        + lax.ppermute(others[1], ("ctx", "resp"), both_moves(ctx_count, resp_count))
    )


def on_device(
    queries,
    attn_cot,
    prompt_latent,
    response_latent,
    log_ratio,
    lengths,
    chosen,
    moe_cot,
    expert_ids,
    router_logits,
    expert_outputs,
):
    ctx_count = lax.axis_size("ctx")
    resp_count = lax.axis_size("resp")
    devices = ctx_count * resp_count
    width = prompt_latent.shape[1]
    tokens, model = moe_cot.shape[1:]
    per_owner = EXPERTS // devices
    start = (lax.axis_index("ctx") * tokens).astype(jnp.int32).reshape(1)
    ids = expert_ids[0].T
    logits = router_logits[0].T

    far_moves = ctx_moves(ctx_count, 1, 0, 0)
    token_rows, slot, table, gates = plan_send(
        lengths, chosen, start, log_ratio, ids, logits, moe_cot[0]
    )
    ring = gather_ring(prompt_latent, ctx_count)
    far = lax.ppermute(prompt_latent, "ctx", far_moves)
    ring, far, token_rows, table, gates = lax.optimization_barrier(
        (ring, far, token_rows, table, gates)
    )
    ring = jnp.concatenate(ring)
    far_ring = lax.ppermute(ring, "ctx", far_moves)
    sent = build_send(table, gates, token_rows, tokens)
    sent, ring, far, far_ring = lax.optimization_barrier((sent, ring, far, far_ring))
    around = jnp.concatenate([prompt_latent, ring, far, far_ring])
    other = lax.ppermute(around, "ctx", ctx_moves(ctx_count, 0, 0, 1))
    arrived = lax.all_to_all(
        unflat(sent, devices, per_owner, CAP, model), ("ctx", "resp"), 0, 0, tiled=True
    )

    grad_query, keep, send = attention(
        lengths, chosen, ctx_places(ctx_count), log_ratio, queries[0], attn_cot[0],
        jnp.concatenate([around, other]), response_latent[0].T,
    )
    held = reduce_over_cores(keep, send, ctx_count)
    around = ring_terms(held, ctx_count)
    terms, rows = slot_dots(flat(arrived), flat(expert_outputs), devices, per_owner)
    around, terms = lax.optimization_barrier((around, terms))
    mine = sum(part.astype(f32) for part in around)
    returned = lax.all_to_all(terms, ("ctx", "resp"), 0, 0, tiled=True)
    prompt_rows = prompt_latent.shape[0]
    grad_response = reduce_answer(mine[:, prompt_rows:], ctx_count)[None]
    parts, my_far = prompt_terms(mine[:, :prompt_rows], resp_count)
    blocks = sum(parts)
    returned, _ = lax.optimization_barrier((returned, blocks))
    grad_prompt = reduce_prompt_far(blocks, my_far, ctx_count, resp_count)

    grad_router = router_grad(returned, ids, slot, logits)
    expert_row_grads = unflat(rows, devices, per_owner, CAP, model)
    return (grad_query[None], grad_prompt, grad_response, expert_row_grads, grad_router.T[None])


def solution(mesh):
    placed = (
        P("resp", None, "ctx"),
        P("resp", None, "ctx"),
        P("ctx", None),
        P("resp", None, None),
        P("resp", None),
        P("resp", None),
        P("resp"),
        P("resp", "ctx", None),
        P("resp", "ctx", None),
        P("resp", "ctx", None),
        P(None, ("ctx", "resp"), None, None),
    )
    return jax.shard_map(
        on_device,
        mesh=mesh,
        in_specs=placed,
        out_specs=(
            P("resp", None, "ctx"),
            P(("ctx", "resp"), None),
            P("resp", "ctx", None),
            P(None, ("ctx", "resp"), None, None),
            P("resp", "ctx", None),
        ),
        check_vma=False,
    )
```

```python
import jax
import jax.numpy as jnp
from jax import lax
from jax.experimental import pallas as pl
from jax.experimental.pallas import tpu as pltpu
from jax.sharding import PartitionSpec as P

EXPERTS = 256
CAP = 2
LANES = 128
PLACED = 4
VMEM = 58 << 20

score_scale = 192.0 ** (-0.5)
preference_beta = 0.5
route_scale = 2.5
log2_e = 1.4426950408889634

f32 = jnp.float32
bf16 = jnp.bfloat16


def coefficient_row(ratio_ref, lengths_ref, chosen_ref):
    rows = ratio_ref.shape[1]
    half = rows // 2
    lane = lax.broadcasted_iota(jnp.int32, (1, rows), 1)
    second = lane >= half
    position = jnp.where(second, lane - half, lane)
    length = jnp.where(second, lengths_ref[0, 1], lengths_ref[0, 0])
    live = position < length
    ratios = jnp.where(live, ratio_ref[...], 0.0)
    first_total = jnp.sum(jnp.where(second, 0.0, ratios), axis=1, keepdims=True)
    second_total = jnp.sum(jnp.where(second, ratios, 0.0), axis=1, keepdims=True)
    chosen = chosen_ref[0]
    margin = first_total - second_total
    margin = jnp.where(chosen == 0, margin, -margin)
    weight = preference_beta * jax.nn.sigmoid(-preference_beta * margin)
    signed = jnp.where(second == (chosen == 1), -weight, weight)
    return jnp.where(live, signed, 0.0)


def column_of(row):
    n = row.shape[1]
    return jnp.transpose(jnp.broadcast_to(row, (8, n)))[:, :1]


def router_gates(logits):
    affinity = jax.nn.sigmoid(logits)
    total = jnp.sum(affinity, axis=0, keepdims=True)
    return affinity, total, route_scale * affinity / total


def plan_kernel(
    lengths_ref, chosen_ref, start_ref, ratio_ref, ids_ref, logits_ref, cot_ref,
    rows_ref, slot_ref, table_ref, gates_ref,
):
    tokens, model = cot_ref.shape
    top = ids_ref.shape[0]
    tiles = model // LANES
    _, _, gate = router_gates(logits_ref[...])
    gate = gate.astype(bf16).astype(f32)
    ids = jnp.transpose(ids_ref[...])
    gates = jnp.transpose(gate)
    expert = lax.broadcasted_iota(jnp.int32, (tokens, EXPERTS), 1)
    named = jnp.zeros((tokens, EXPERTS), f32)
    weight = jnp.zeros((tokens, EXPERTS), f32)
    for n in range(top):
        hit = ids[:, n : n + 1] == expert
        named = jnp.where(hit, 1.0, named)
        weight = jnp.where(hit, gates[:, n : n + 1], weight)
    row_i = lax.broadcasted_iota(jnp.int32, (tokens, tokens), 0)
    col_i = lax.broadcasted_iota(jnp.int32, (tokens, tokens), 1)
    before = jnp.dot((col_i < row_i).astype(bf16), named.astype(bf16), preferred_element_type=f32)
    token = lax.broadcasted_iota(jnp.int32, (tokens, EXPERTS), 0).astype(f32)
    for s in range(CAP):
        here = jnp.where((before == float(s)) & (named > 0.0), 1.0, 0.0)
        table_ref[s : s + 1, :] = jnp.sum(here * token, axis=0, keepdims=True).astype(jnp.int32)
        gates_ref[s : s + 1, :] = jnp.sum(here * weight, axis=0, keepdims=True)
    slots = []
    for n in range(top):
        hit = ids[:, n : n + 1] == expert
        slots.append(jnp.sum(jnp.where(hit, before, 0.0), axis=1, keepdims=True))
    slot_ref[...] = jnp.transpose(jnp.concatenate(slots, axis=1)).astype(jnp.int32)
    coefficient = coefficient_row(ratio_ref, lengths_ref, chosen_ref)
    lane = lax.broadcasted_iota(jnp.int32, (tokens, coefficient.shape[1]), 1)
    row = lax.broadcasted_iota(jnp.int32, (tokens, coefficient.shape[1]), 0)
    own = jnp.sum(jnp.where(lane == row + start_ref[0], coefficient, 0.0), axis=1, keepdims=True)
    for tile in range(tiles):
        cot = cot_ref[:, tile * LANES : (tile + 1) * LANES].astype(f32)
        rows_ref[pl.ds(tile, tokens, stride=tiles), :] = (own * cot).astype(bf16).astype(f32)


def plan_send(lengths, chosen, start, ratio, ids, logits, cot):
    tokens, model = cot.shape
    smem = pl.BlockSpec(memory_space=pltpu.SMEM)
    vmem = pl.BlockSpec(memory_space=pltpu.VMEM)
    return pl.pallas_call(
        plan_kernel,
        in_specs=[smem, smem, smem, vmem, vmem, vmem, vmem],
        out_specs=[vmem, vmem, vmem, vmem],
        out_shape=[
            jax.ShapeDtypeStruct((tokens * (model // LANES), LANES), f32),
            jax.ShapeDtypeStruct(ids.shape, jnp.int32),
            jax.ShapeDtypeStruct((CAP, EXPERTS), jnp.int32),
            jax.ShapeDtypeStruct((CAP, EXPERTS), f32),
        ],
        compiler_params=pltpu.CompilerParams(vmem_limit_bytes=VMEM),
        cost_estimate=pl.CostEstimate(flops=0, bytes_accessed=1_500_000, transcendentals=0),
        name="plan_send",
    )(lengths, chosen, start, ratio, ids, logits, cot)


def send_kernel(table_ref, gates_ref, rows_ref, send_hbm, pair_ref, send_ref, send_sems):
    tiles = pair_ref.shape[1] // CAP
    parts = send_sems.shape[0]
    per_part = EXPERTS // parts
    part_rows = per_part * tiles * CAP

    def place(group, carry):
        for u in range(PLACED):
            e = group * PLACED + u
            for s in range(CAP):
                token = table_ref[s, e]
                block = rows_ref[pl.ds(pl.multiple_of(token * tiles, 8), tiles), :]
                pair_ref[u, pl.ds(s, tiles, stride=CAP), :] = block * gates_ref[s, e]
        for u in range(PLACED):
            at = pl.multiple_of((group * PLACED + u) * (tiles * CAP), 16)
            send_ref[pl.ds(at, tiles * CAP), :] = pair_ref[u].astype(bf16)
        return carry

    def send_copy(part):
        at = pl.ds(pl.multiple_of(part * part_rows, 16), part_rows)
        return pltpu.make_async_copy(send_ref.at[at], send_hbm.at[at], send_sems.at[part])

    def one_part(part, carry):
        first = part * (per_part // PLACED)
        lax.fori_loop(0, per_part // PLACED, lambda g, c: place(first + g, c), 0, unroll=2)
        send_copy(part).start()
        return carry

    lax.fori_loop(0, parts, one_part, 0)
    for part in range(parts):
        send_copy(part).wait()


def build_send(table, gates, token_rows, tokens):
    tiles = token_rows.shape[0] // tokens
    rows = EXPERTS * CAP * tiles
    parts = 16
    smem = pl.BlockSpec(memory_space=pltpu.SMEM)
    vmem = pl.BlockSpec(memory_space=pltpu.VMEM)
    return pl.pallas_call(
        send_kernel,
        in_specs=[smem, smem, vmem],
        out_specs=pl.BlockSpec(memory_space=pl.ANY),
        out_shape=jax.ShapeDtypeStruct((rows, LANES), bf16),
        scratch_shapes=[
            pltpu.VMEM((PLACED, tiles * CAP, LANES), f32),
            pltpu.VMEM((rows, LANES), bf16),
            pltpu.SemaphoreType.DMA((parts,)),
        ],
        compiler_params=pltpu.CompilerParams(vmem_limit_bytes=VMEM),
        cost_estimate=pl.CostEstimate(flops=0, bytes_accessed=8_000_000, transcendentals=0),
        name="build_send",
    )(table, gates, token_rows)


def dot_kernel(got_hbm, saved_hbm, out_ref, rows_hbm, got_ref, saved_ref, acc_ref, sems):
    sources = out_ref.shape[0]
    per_owner = EXPERTS // sources
    parts = sems.shape[1]
    rows = got_ref.shape[0] // parts
    owners = sources // parts
    tall = rows // (owners * per_owner)

    def copies(part):
        at = pl.ds(pl.multiple_of(part * rows, 16), rows)
        return (
            pltpu.make_async_copy(got_hbm.at[at], got_ref.at[at], sems.at[0, part]),
            pltpu.make_async_copy(saved_hbm.at[at], saved_ref.at[at], sems.at[1, part]),
        )

    def pass_on(part):
        at = pl.ds(pl.multiple_of(part * rows, 16), rows)
        return pltpu.make_async_copy(got_ref.at[at], rows_hbm.at[at], sems.at[2, part])

    for part in range(parts):
        for copy in copies(part):
            copy.start()

    def work(part, carry):
        for copy in copies(part):
            copy.wait()
        pass_on(part).start()
        for p in range(owners * per_owner):
            at = pl.ds(pl.multiple_of(part * rows + p * tall, 16), tall)
            product = got_ref[at, :].astype(f32) * saved_ref[at, :].astype(f32)
            acc_ref[p] = jnp.sum(product.reshape(tall // 8, 8, LANES), axis=0)
        product = acc_ref[...].reshape(owners, per_owner, 8, LANES)
        spare = jnp.zeros((owners, LANES - 8 * per_owner), f32)
        out_ref[pl.ds(pl.multiple_of(part * owners, 8), owners), :] = jnp.concatenate(
            [jnp.sum(product[:, e], axis=2) for e in range(per_owner)] + [spare], axis=1
        )
        return carry

    lax.fori_loop(0, parts, work, 0)
    for part in range(parts):
        pass_on(part).wait()


def slot_dots(got, saved, sources, per_owner):
    parts = 16
    anywhere = pl.BlockSpec(memory_space=pl.ANY)
    return pl.pallas_call(
        dot_kernel,
        in_specs=[anywhere, anywhere],
        out_specs=[pl.BlockSpec(memory_space=pltpu.VMEM), anywhere],
        out_shape=[
            jax.ShapeDtypeStruct((sources, LANES), f32),
            jax.ShapeDtypeStruct(got.shape, got.dtype),
        ],
        scratch_shapes=[
            pltpu.VMEM(got.shape, got.dtype),
            pltpu.VMEM(got.shape, got.dtype),
            pltpu.VMEM((sources // parts * per_owner, 8, LANES), f32),
            pltpu.SemaphoreType.DMA((3, parts)),
        ],
        compiler_params=pltpu.CompilerParams(vmem_limit_bytes=VMEM),
        cost_estimate=pl.CostEstimate(flops=8_000_000, bytes_accessed=15_000_000, transcendentals=0),
        name="slot_dots",
    )(got, saved)


def router_kernel(terms_ref, ids_ref, slot_ref, logits_ref, out_ref):
    top, tokens = ids_ref.shape
    owners = terms_ref.shape[0]
    per_owner = EXPERTS // owners
    affinity, total, gate = router_gates(logits_ref[...])
    ids = jnp.transpose(ids_ref[...])
    slots = jnp.transpose(slot_ref[...])
    terms = jnp.transpose(terms_ref[...])
    owner = lax.broadcasted_iota(jnp.int32, (tokens, owners), 1)
    columns = []
    for n in range(top):
        expert = ids[:, n : n + 1]
        slot = slots[:, n : n + 1]
        picked = jnp.zeros((tokens, owners), f32)
        for e in range(per_owner):
            for s in range(CAP):
                dot = jnp.zeros((1, owners), f32)
                for k in range(s, 8, CAP):
                    dot = dot + terms[e * 8 + k : e * 8 + k + 1]
                hit = (owner * per_owner + e == expert) & (slot == s)
                picked = jnp.where(hit, dot, picked)
        columns.append(jnp.sum(picked, axis=1, keepdims=True))
    gate_grad = jnp.transpose(jnp.concatenate(columns, axis=1)) / gate.astype(bf16).astype(f32)
    mixed = jnp.sum(gate_grad * affinity, axis=0, keepdims=True) / total
    out_ref[...] = route_scale / total * (gate_grad - mixed) * affinity * (1.0 - affinity)


def router_grad(terms, ids, slot, logits):
    return pl.pallas_call(
        router_kernel,
        out_shape=jax.ShapeDtypeStruct(logits.shape, f32),
        compiler_params=pltpu.CompilerParams(vmem_limit_bytes=VMEM),
        name="router_grad",
    )(terms, ids, slot, logits)


NT = (((1,), (1,)), ((), ()))


def attention_kernel(
    lengths_ref, chosen_ref, place_ref, ratio_ref, q_ref, cot_ref, prompt_ref, answer_ref,
    gq_ref, keep_ref, send_ref, keys_ref, keys_t_ref, acc_ref, value_ref,
):
    prompt_count, width = prompt_ref.shape
    row_count = answer_ref.shape[1]
    half = row_count // 2
    wide = keys_ref.shape[2]
    rank = value_ref.shape[1]
    pad = wide - width
    step = pl.program_id(0)

    @pl.when(step == 0)
    def _():
        answer_t = answer_ref[...]
        keys_t_ref[:, :prompt_count] = jnp.transpose(prompt_ref[...])
        keys_t_ref[:, prompt_count:] = answer_t
        latent = jnp.concatenate([prompt_ref[...], jnp.transpose(answer_t)], axis=0)
        zeros = jnp.zeros((latent.shape[0], pad), bf16)
        keys_ref[0] = jnp.concatenate([latent, zeros], axis=1)
        keys_ref[1] = jnp.concatenate([zeros, latent], axis=1)
        acc_ref[...] = jnp.zeros_like(acc_ref)
        value_ref[...] = jnp.zeros_like(value_ref)

    coefficient = column_of(coefficient_row(ratio_ref, lengths_ref, chosen_ref))
    key_i = lax.broadcasted_iota(jnp.int32, (half, half), 0)
    row_i = lax.broadcasted_iota(jnp.int32, (half, half), 1)
    causal = key_i <= row_i
    for k in range(2):
        rows = slice(k * half, (k + 1) * half)
        answer = slice(prompt_count + k * half, prompt_count + (k + 1) * half)
        grads = []
        for h in range(2):
            query = q_ref[rows, h * rank : h * rank + wide]
            grad_out = (
                coefficient[rows] * cot_ref[rows, h * rank : (h + 1) * rank].astype(f32)
            ).astype(bf16)
            s_prompt = lax.dot_general(
                keys_ref[h, :prompt_count], query, NT, preferred_element_type=f32
            )
            s_answer = lax.dot_general(keys_ref[h, answer], query, NT, preferred_element_type=f32)
            s_answer = jnp.where(causal, s_answer, -1e30)
            top = jnp.maximum(
                jnp.max(s_prompt, axis=0, keepdims=True), jnp.max(s_answer, axis=0, keepdims=True)
            )
            e_prompt = jnp.exp2((s_prompt - top) * (score_scale * log2_e))
            e_answer = jnp.exp2((s_answer - top) * (score_scale * log2_e))
            total = jnp.sum(e_prompt, axis=0, keepdims=True) + jnp.sum(
                e_answer, axis=0, keepdims=True
            )
            inverse = 1.0 / total
            p_prompt = e_prompt * inverse
            p_answer = e_answer * inverse
            b_prompt = p_prompt.astype(bf16)
            b_answer = p_answer.astype(bf16)
            d_prompt = lax.dot_general(
                keys_ref[0, :prompt_count, :rank], grad_out, NT, preferred_element_type=f32
            )
            d_answer = lax.dot_general(
                keys_ref[0, answer, :rank], grad_out, NT, preferred_element_type=f32
            )
            delta = jnp.sum(b_prompt.astype(f32) * d_prompt, axis=0, keepdims=True) + jnp.sum(
                b_answer.astype(f32) * d_answer, axis=0, keepdims=True
            )
            g_prompt = (p_prompt * (d_prompt - delta)).astype(bf16)
            g_answer = (p_answer * (d_answer - delta)).astype(bf16)
            grads.append(
                jnp.dot(keys_t_ref[:, :prompt_count], g_prompt, preferred_element_type=f32)
                + jnp.dot(keys_t_ref[:, answer], g_answer, preferred_element_type=f32)
            )
            acc_ref[h, :prompt_count] += jnp.dot(g_prompt, query, preferred_element_type=f32)
            acc_ref[h, answer] += jnp.dot(g_answer, query, preferred_element_type=f32)
            value_ref[:prompt_count] += jnp.dot(b_prompt, grad_out, preferred_element_type=f32)
            value_ref[answer] += jnp.dot(b_answer, grad_out, preferred_element_type=f32)
        both = (score_scale * jnp.concatenate(grads, axis=0)).astype(bf16)
        gq_ref[rows, :] = jnp.transpose(both)

    @pl.when(step == pl.num_programs(0) - 1)
    def _():
        half_chunks = send_ref.shape[0]
        prompt_rows = prompt_count // (2 * half_chunks)
        answer_rows = row_count // (2 * half_chunks)

        def combined(at):
            size = at.size
            key = acc_ref[0, at, :width] + pltpu.roll(acc_ref[1, at, :], wide - pad, 1)[:, :width]
            value = jnp.concatenate([value_ref[at, :], jnp.zeros((size, width - rank), f32)], axis=1)
            return (score_scale * key + value).astype(bf16)

        for side, out in enumerate((keep_ref, send_ref)):
            for c in range(half_chunks):
                chunk = side * half_chunks + c
                out[c, :prompt_rows] = combined(pl.ds(chunk * prompt_rows, prompt_rows))
                at = pl.multiple_of(prompt_count + place_ref[chunk] * answer_rows, answer_rows)
                out[c, prompt_rows:] = combined(pl.ds(at, answer_rows))


def attention(lengths, chosen, place, ratio, queries, cot, prompt, answer_t):
    rows, q_width = queries.shape
    prompt_count, width = prompt.shape
    heads = q_width // width
    rank = cot.shape[1] // heads
    wide = width + width - rank
    steps = heads // 2
    keys = prompt_count + rows
    chunks = place.shape[0]
    part = (chunks // 2, keys // chunks, width)
    whole = lambda shape: pl.BlockSpec(shape, lambda i: (0,) * len(shape))
    smem = pl.BlockSpec(memory_space=pltpu.SMEM)
    return pl.pallas_call(
        attention_kernel,
        grid=(steps,),
        in_specs=[
            smem, smem, smem, whole(ratio.shape),
            pl.BlockSpec((rows, 2 * width), lambda i: (0, i)),
            pl.BlockSpec((rows, 2 * rank), lambda i: (0, i)),
            whole(prompt.shape), whole(answer_t.shape),
        ],
        out_specs=[
            pl.BlockSpec((rows, 2 * width), lambda i: (0, i)),
            whole(part),
            whole(part),
        ],
        out_shape=[
            jax.ShapeDtypeStruct(queries.shape, bf16),
            jax.ShapeDtypeStruct(part, bf16),
            jax.ShapeDtypeStruct(part, bf16),
        ],
        scratch_shapes=[
            pltpu.VMEM((2, keys, wide), bf16),
            pltpu.VMEM((width, keys), bf16),
            pltpu.VMEM((2, keys, wide), f32),
            pltpu.VMEM((keys, rank), f32),
        ],
        compiler_params=pltpu.CompilerParams(vmem_limit_bytes=VMEM),
        cost_estimate=pl.CostEstimate(
            flops=17_000_000_000, bytes_accessed=9_000_000, transcendentals=2_600_000
        ),
        name="attention",
    )(lengths, chosen, place, ratio, queries, cot, prompt, answer_t)


def flat(x):
    n, e, s, d = x.shape
    t = d // LANES
    return x.reshape(n, e, s, t, LANES).transpose(0, 1, 3, 2, 4).reshape(n * e * t * s, LANES)


def unflat(x, n, e, s, d):
    t = d // LANES
    return x.reshape(n, e, t, s, LANES).transpose(0, 1, 3, 2, 4).reshape(n, e, s, d)


def ctx_moves(count, far, ring, core):
    rings = count // 4
    moves = []
    for f in range(2):
        for r in range(rings):
            for c in range(2):
                source = (f * rings + r) * 2 + c
                moves.append((source, ((f ^ far) * rings + (r + ring) % rings) * 2 + (c ^ core)))
    return moves


def resp_moves(count, ring, far):
    rings = count // 2
    return [
        (r * 2 + f, (r + ring) % rings * 2 + (f ^ far)) for r in range(rings) for f in range(2)
    ]


def gather_ring(rows, count):
    rings = count // 4
    return [lax.ppermute(rows, "ctx", ctx_moves(count, 0, rings - d, 0)) for d in range(1, rings)]


def ctx_places(count):
    rings = count // 4
    me = lax.axis_index("ctx")
    order = jnp.arange(count, dtype=jnp.int32)
    core, far, ring = order // (rings * 2), order // rings % 2, order % rings
    my_core, my_ring, my_far = me % 2, me // 2 % rings, me // (rings * 2)
    return ((my_far ^ far) * rings + (my_ring + ring) % rings) * 2 + (my_core ^ core)


def reduce_over_cores(keep, send, count):
    got = lax.ppermute(send, "ctx", ctx_moves(count, 0, 0, 1))
    return (keep.astype(f32) + got.astype(f32)).reshape((2, count // 4) + keep.shape[1:])


def both_moves(ctx_count, resp_count):
    return [
        (c0 * resp_count + r0, c1 * resp_count + r1)
        for c0, c1 in ctx_moves(ctx_count, 1, 0, 0)
        for r0, r1 in resp_moves(resp_count, 0, 1)
    ]


def ring_terms(held, count):
    low = held.astype(bf16)
    return [held[:, 0]] + [
        lax.ppermute(low[:, d], "ctx", ctx_moves(count, 0, d, 0)) for d in range(1, count // 4)
    ]


def reduce_answer(rows, count):
    return rows[0] + lax.ppermute(rows[1], "ctx", ctx_moves(count, 1, 0, 0))


def prompt_terms(rows, resp_count):
    rings = resp_count // 2
    me = lax.axis_index("resp")
    my_ring, my_far = me // 2, me % 2
    blocks = rows.reshape(2, rings, 2, rows.shape[1] // resp_count, rows.shape[2])
    twice = jnp.concatenate([blocks, blocks[:, : rings - 1]], axis=1)
    blocks = lax.dynamic_slice_in_dim(twice, my_ring, rings, axis=1)
    parts = [blocks[:, 0]] + [
        lax.ppermute(blocks[:, d], "resp", resp_moves(resp_count, d, 0)) for d in range(1, rings)
    ]
    return parts, my_far


def reduce_prompt_far(mine, my_far, ctx_count, resp_count):
    own = lax.dynamic_index_in_dim(mine, my_far, axis=1, keepdims=False)
    others = lax.dynamic_index_in_dim(mine, 1 - my_far, axis=1, keepdims=False)
    return (
        own[0]
        + lax.ppermute(own[1], "ctx", ctx_moves(ctx_count, 1, 0, 0))
        + lax.ppermute(others[0], "resp", resp_moves(resp_count, 0, 1))
        + lax.ppermute(others[1], ("ctx", "resp"), both_moves(ctx_count, resp_count))
    )


def on_device(
    queries,
    attn_cot,
    prompt_latent,
    response_latent,
    log_ratio,
    lengths,
    chosen,
    moe_cot,
    expert_ids,
    router_logits,
    expert_outputs,
):
    ctx_count = lax.axis_size("ctx")
    resp_count = lax.axis_size("resp")
    devices = ctx_count * resp_count
    width = prompt_latent.shape[1]
    tokens, model = moe_cot.shape[1:]
    per_owner = EXPERTS // devices
    start = (lax.axis_index("ctx") * tokens).astype(jnp.int32).reshape(1)
    ids = expert_ids[0].T
    logits = router_logits[0].T

    far_moves = ctx_moves(ctx_count, 1, 0, 0)
    token_rows, slot, table, gates = plan_send(
        lengths, chosen, start, log_ratio, ids, logits, moe_cot[0]
    )
    ring = gather_ring(prompt_latent, ctx_count)
    far = lax.ppermute(prompt_latent, "ctx", far_moves)
    ring, far, token_rows, table, gates = lax.optimization_barrier(
        (ring, far, token_rows, table, gates)
    )
    ring = jnp.concatenate(ring)
    far_ring = lax.ppermute(ring, "ctx", far_moves)
    sent = build_send(table, gates, token_rows, tokens)
    sent, ring, far, far_ring = lax.optimization_barrier((sent, ring, far, far_ring))
    around = jnp.concatenate([prompt_latent, ring, far, far_ring])
    other = lax.ppermute(around, "ctx", ctx_moves(ctx_count, 0, 0, 1))
    arrived = lax.all_to_all(
        unflat(sent, devices, per_owner, CAP, model), ("ctx", "resp"), 0, 0, tiled=True
    )

    grad_query, keep, send = attention(
        lengths, chosen, ctx_places(ctx_count), log_ratio, queries[0], attn_cot[0],
        jnp.concatenate([around, other]), response_latent[0].T,
    )
    held = reduce_over_cores(keep, send, ctx_count)
    around = ring_terms(held, ctx_count)
    terms, rows = slot_dots(flat(arrived), flat(expert_outputs), devices, per_owner)
    around, terms = lax.optimization_barrier((around, terms))
    mine = sum(part.astype(f32) for part in around)
    returned = lax.all_to_all(terms, ("ctx", "resp"), 0, 0, tiled=True)
    prompt_rows = prompt_latent.shape[0]
    grad_response = reduce_answer(mine[:, prompt_rows:], ctx_count)[None]
    parts, my_far = prompt_terms(mine[:, :prompt_rows], resp_count)
    blocks = sum(parts)
    returned, _ = lax.optimization_barrier((returned, blocks))
    grad_prompt = reduce_prompt_far(blocks, my_far, ctx_count, resp_count)

    grad_router = router_grad(returned, ids, slot, logits)
    expert_row_grads = unflat(rows, devices, per_owner, CAP, model)
    return (grad_query[None], grad_prompt, grad_response, expert_row_grads, grad_router.T[None])


def solution(mesh):
    placed = (
        P("resp", None, "ctx"),
        P("resp", None, "ctx"),
        P("ctx", None),
        P("resp", None, None),
        P("resp", None),
        P("resp", None),
        P("resp"),
        P("resp", "ctx", None),
        P("resp", "ctx", None),
        P("resp", "ctx", None),
        P(None, ("ctx", "resp"), None, None),
    )
    return jax.shard_map(
        on_device,
        mesh=mesh,
        in_specs=placed,
        out_specs=(
            P("resp", None, "ctx"),
            P(("ctx", "resp"), None),
            P("resp", "ctx", None),
            P(None, ("ctx", "resp"), None, None),
            P("resp", "ctx", None),
        ),
        check_vma=False,
    )
```
